256 devices in a mesh: section: 16 (over z_lo, y, core), enc: 16 (over z_hi, x).
Axes of the slice: x: 4, y: 4, z: 8 (z_hi: 4, z_lo: 2; z = z_hi * 2 + z_lo), core: 2. Of those that a mesh axis runs over, the one named last changes fastest.
Arguments:
- latents: bfloat16 [48, 64, 1280], P('enc', 'section'), may hold values from -4 to 4
- key_weight: bfloat16 [16, 1280, 4096], P('section', None, 'enc'), may hold values from -0.1118034 to 0.1118034
- value_weight: bfloat16 [16, 1280, 4096], P('section', None, 'enc'), may hold values from -0.15625 to 0.15625
- gate_logit: float32 [16], P('section'), may hold values from 0.3 to 1.5
- queries: bfloat16 [16, 1024, 4096], P('section', None, 'enc'), may hold values from -150 to 150
- cotangent: bfloat16 [16, 1024, 4096], P('section', None, 'enc'), may hold values from -6 to 6
- image_counts: int32 [16], replicated, may hold values from 1 to 3, as said below
- token_image: int32 [1024], replicated, may hold values from 0 to 31, as said below
Outputs:
- attended: bfloat16 [16, 1024, 4096], P('section', None, 'enc')
- grad_queries: bfloat16 [16, 1024, 4096], P('section', None, 'enc')
- grad_latents: float32 [48, 64, 1280], P('enc', 'section')
The draws below stay inside these ranges and needn't reach their ends.
Inputs may be any that keep to these rules, and one draw needn't show every extreme that they name: `image_counts`: the images of all owners sum to 32. `token_image`: never falls along the tokens; every image has at least 8 tokens, and some image exactly that many.
All inputs are finite; a program needn't handle non-finite values.
Results may differ from the reference program's by a relative error of at most 0.028.
Values may be sent and summed in bfloat16 or wider, within the bound.
A program may use at most 128 MiB of HBM per device.

```python
import math
import jax
import jax.numpy as jnp
from jax import lax

VD = 1280
LAT = 64
HEADS = 32
HD = 128
IMG_DEV = 2
IMG_CAP = 3
TXT_IMG = 32
SECTIONS = 16
OWNERS = 16
IMAGES = 32
SLOTS = 48
TOKENS = 1024


def shared_counts(key):
    key = jax.random.fold_in(key, 11)
    first_key, second_key = jax.random.split(key)
    ranking = jax.random.permutation(first_key, OWNERS)
    shifted = jax.random.randint(second_key, (), 1, OWNERS // 2 + 1)
    change = jnp.where(ranking < shifted, 1, jnp.where(ranking < 2 * shifted, -1, 0))
    return (IMG_DEV + change * (IMG_CAP - IMG_DEV)).astype(jnp.int32)


def shared_tokens(key):
    key = jax.random.fold_in(key, 12)
    first_key, second_key = jax.random.split(key)
    ranking = jax.random.permutation(first_key, IMAGES)
    spread = jax.random.randint(second_key, (IMAGES // 2,), 0, TXT_IMG * 3 // 4 + 1)
    spread = spread.at[0].set(TXT_IMG * 3 // 4)
    direction = jnp.where(ranking % 2 == 0, 1, -1)
    lengths = TXT_IMG + direction * spread[ranking // 2]
    image_ends = jnp.cumsum(lengths)
    position = jnp.arange(TOKENS)
    return jnp.sum((position[:, None] >= image_ends[None, :]).astype(jnp.int32), axis=1).astype(jnp.int32)


def shared_latents(key):
    key = jax.random.fold_in(key, 13)
    return jax.random.truncated_normal(key, -4.0, 4.0, (SLOTS, LAT, VD), jnp.float32)


def shared_keys(key):
    key = jax.random.fold_in(key, 14)
    return jax.random.truncated_normal(key, -3.96, 3.96, (SECTIONS, VD, HEADS * HD), jnp.float32) * VD ** (-0.5)


def draw_latents(key, part):
    drawn = shared_latents(key)
    return drawn.astype(jnp.bfloat16)


def draw_key_weight(key, part):
    drawn = shared_keys(key)
    return drawn.astype(jnp.bfloat16)


def draw_image_counts(key, part):
    drawn = shared_counts(key)
    return drawn


def draw_token_image(key, part):
    drawn = shared_tokens(key)
    return drawn


def draw_queries(key, part):
    key = jax.random.fold_in(key, 5)
    return jax.random.normal(key, (SECTIONS, TOKENS, HEADS * HD), jnp.float32).astype(jnp.bfloat16)


def block_scale(rng, dims, cuts, smallest, top_value):
    def one(axis_at, blocks):
        heights = jax.random.uniform(jax.random.fold_in(jax.random.fold_in(rng, 6), axis_at), (blocks,), jnp.float32, smallest / len(cuts), top_value / len(cuts))
        return jnp.repeat(jnp.exp(heights), dims[axis_at] // blocks).reshape((-1,) + (1,) * (len(dims) - axis_at - 1))

    level = one(*cuts[0])
    for cut in cuts[1:]:
        level = level * one(*cut)
    return level


def scatter_about(key, shape, scale, reach, cuts=(), kind=jnp.bfloat16):
    values = scale * jax.random.normal(key, shape, jnp.float32)
    if cuts:
        values = values * block_scale(key, shape, cuts, -0.22, 0.18)
    return jnp.clip(values, -reach, reach).astype(kind)


def setup_inputs(seed: int = 0) -> dict:
    key_list = jax.random.split(jax.random.key(seed), 9)
    latents = draw_latents(jax.random.fold_in(key_list[8], 71), 0)
    key_weight = draw_key_weight(jax.random.fold_in(key_list[8], 71), 0)
    value_weight = scatter_about(key_list[2], (SECTIONS, VD, HEADS * HD), VD ** -0.5, 0.15625, ((0, 16), (2, 16)))
    gate_logit = jnp.clip(0.3 + 1.2 * jax.random.uniform(key_list[3], (SECTIONS,), jnp.float32) ** block_scale(key_list[3], (SECTIONS,), ((0, 16),), -0.2, 0.2), 0.3, 1.5)
    queries = draw_queries(jax.random.fold_in(key_list[8], 71), 0)
    cotangent = scatter_about(key_list[5], (SECTIONS, TOKENS, HEADS * HD), 1.0, 6.0, ((0, 16), (2, 16)))
    image_counts = draw_image_counts(jax.random.fold_in(key_list[8], 71), 0)
    token_image = draw_token_image(jax.random.fold_in(key_list[8], 71), 0)
    return {"latents": latents, "key_weight": key_weight, "value_weight": value_weight, "gate_logit": gate_logit, "queries": queries, "cotangent": cotangent, "image_counts": image_counts, "token_image": token_image}


def image_slots(image_counts, images, capacity):
    owners = image_counts.shape[0]
    image_ends = jnp.cumsum(image_counts).astype(jnp.int32)
    image_starts = image_ends - image_counts
    image_index = jnp.arange(images, dtype=jnp.int32)
    owner_of = lax.optimization_barrier(jnp.sum((image_index[:, None] >= image_ends[None, :]).astype(jnp.int32), axis=1))
    owner_match = owner_of[:, None] == jnp.arange(owners, dtype=jnp.int32)[None, :]
    first_image = lax.optimization_barrier(jnp.sum(jnp.where(owner_match, image_starts[None, :], 0), axis=1)).astype(jnp.int32)
    return (owner_of * capacity + image_index - first_image).astype(jnp.int32)

def slot_images(image_counts, capacity):
    image_ends = jnp.cumsum(image_counts).astype(jnp.int32)
    image_starts = image_ends - image_counts
    slot_index = jnp.arange(image_counts.shape[0] * capacity, dtype=jnp.int32)
    slot_place = slot_index % capacity
    counts_of = jnp.repeat(image_counts, capacity)
    starts_of = jnp.repeat(image_starts, capacity)
    occupied = slot_place < counts_of
    return (occupied, jnp.where(occupied, starts_of + slot_place, 0).astype(jnp.int32))

def reference(latents, key_weight, value_weight, gate_logit, queries, cotangent, image_counts, token_image):
    image_slot = image_slots(image_counts, IMAGES, IMG_CAP)
    chosen = latents[image_slot].reshape(IMAGES * LAT, VD)
    score_scale = 1.0 / math.sqrt(HD)
    block_rows = math.gcd(TOKENS, 64)
    block_count = TOKENS // block_rows
    occupied, source_image = slot_images(image_counts, IMG_CAP)
    f32 = jnp.float32

    def section_step(running, section_inputs):
        section_keys, section_values, section_gate, section_queries, section_cot = section_inputs
        key_rows = jnp.dot(chosen, section_keys, preferred_element_type=f32).astype(jnp.bfloat16).reshape(IMAGES, LAT, HEADS, HD)
        value_rows = jnp.dot(chosen, section_values, preferred_element_type=f32).astype(jnp.bfloat16).reshape(IMAGES, LAT, HEADS, HD)
        factor = jnp.tanh(section_gate)

        def token_block(carry, block_inputs):
            grad_keys, grad_values = carry
            query_block, cot_block, image_block = block_inputs
            token_keys = key_rows[image_block].astype(f32)
            token_values = value_rows[image_block].astype(f32)
            scores = jnp.einsum('thd,tshd->ths', query_block.astype(f32), token_keys) * score_scale
            row_max = lax.optimization_barrier(jnp.max(scores, axis=2, keepdims=True))
            exponent = jnp.exp(scores - row_max)
            probs = exponent / lax.optimization_barrier(jnp.sum(exponent, axis=2, keepdims=True))
            probs_b = probs.astype(jnp.bfloat16)
            mixture = jnp.einsum('ths,tshd->thd', probs_b.astype(f32), token_values)
            attended = (factor * mixture).astype(jnp.bfloat16)
            grad_mix = (factor * cot_block.astype(f32)).astype(jnp.bfloat16)
            grad_probs = jnp.einsum('thd,tshd->ths', grad_mix.astype(f32), token_values)
            weighted = lax.optimization_barrier(jnp.sum(probs * grad_probs, axis=2, keepdims=True))
            grad_scores = (probs * (grad_probs - weighted) * score_scale).astype(jnp.bfloat16)
            grad_query = jnp.einsum('ths,tshd->thd', grad_scores.astype(f32), token_keys).astype(jnp.bfloat16)
            grad_keys = grad_keys.at[image_block].add(jnp.einsum('ths,thd->tshd', grad_scores.astype(f32), query_block.astype(f32)))
            grad_values = grad_values.at[image_block].add(jnp.einsum('ths,thd->tshd', probs_b.astype(f32), grad_mix.astype(f32)))
            return ((grad_keys, grad_values), (attended, grad_query))
        zeros = jnp.zeros((IMAGES, LAT, HEADS, HD), f32)
        block_inputs = (section_queries.reshape(block_count, block_rows, HEADS, HD), section_cot.reshape(block_count, block_rows, HEADS, HD), token_image.reshape(block_count, block_rows))
        (grad_keys, grad_values), (attended, grad_query) = lax.scan(token_block, (zeros, zeros), block_inputs)
        grad_keys = grad_keys.astype(jnp.bfloat16).reshape(IMAGES * LAT, HEADS * HD)
        grad_values = grad_values.astype(jnp.bfloat16).reshape(IMAGES * LAT, HEADS * HD)
        contract = (((1,), (1,)), ((), ()))
        section_term = lax.dot_general(grad_keys, section_keys, contract, preferred_element_type=f32)
        section_term = section_term + lax.dot_general(grad_values, section_values, contract, preferred_element_type=f32)
        return (running + section_term, (attended.reshape(TOKENS, HEADS * HD), grad_query.reshape(TOKENS, HEADS * HD)))
    initial = jnp.zeros((IMAGES * LAT, VD), f32)
    running, (attended, grad_queries) = lax.scan(section_step, initial, (key_weight, value_weight, gate_logit, queries, cotangent))
    per_image = running.reshape(IMAGES, LAT, VD)
    grad_latents = jnp.where(occupied[:, None, None], per_image[source_image], jnp.zeros((), f32))
    return (attended, grad_queries, grad_latents)
```

```python
import math

import jax
import jax.numpy as jnp
from jax import lax
from jax.experimental import pallas as pl
from jax.experimental.pallas import tpu as pltpu
from jax.sharding import PartitionSpec as P

HD = 128
CAP = 3
NX, NY, NZ = 4, 4, 8
MESH = pl.DeviceIdType.MESH
f32 = jnp.float32
bf16 = jnp.bfloat16


def place():
    section = lax.axis_index("section")
    enc = lax.axis_index("enc")
    x = lax.rem(enc, NX)
    y = lax.rem(section // 2, NY)
    z = (enc // NX) * 2 + section // (2 * NY)
    return x, y, z, lax.rem(section, 2)


def device(x, y, z, c):
    return (lax.rem(z, 2) * (2 * NY) + y * 2 + c, (z // 2) * NX + x)


def turn(a, d, n):
    return lax.rem(a + d + n, n)


class Links:
    def __init__(self, send_sem, recv_sem):
        self.send_sem, self.recv_sem = send_sem, recv_sem
        self.used = 0
        self.sent = []

    def send(self, src, dst, dev):
        i = self.used
        self.used += 1
        copy = pltpu.make_async_remote_copy(
            src_ref=src,
            dst_ref=dst,
            send_sem=self.send_sem.at[i],
            recv_sem=self.recv_sem.at[i],
            device_id=dev,
            device_id_type=MESH,
        )
        copy.start()
        self.sent.append(copy)
        return copy

    def finish(self):
        for copy in self.sent:
            copy.wait_send()


def enter(x, y, z, c):
    peers = [device(x, turn(y, d, NY), z, c) for d in (1, 2, 3)]
    peers += [device(turn(x, d, NX), y, z, c) for d in (1, -1)]
    peers += [device(x, y, turn(z, d, NZ), c) for d in (1, -1)]
    peers += [device(x, y, z, 1 - c)]
    barrier = pltpu.get_barrier_semaphore()
    for peer in peers:
        pl.semaphore_signal(barrier, inc=1, device_id=peer, device_id_type=MESH)
    pl.semaphore_wait(barrier, len(peers))


GATHER_SEMS = 160


def gather_kernel(
    own_ref, kw_ref, vw_ref, all_ref, kws_ref, vws_ref, held, column, rows, send_sem, recv_sem, local_sem
):
    x, y, z, c = place()
    links = Links(send_sem, recv_sem)
    right, left = device(turn(x, 1, NX), y, z, c), device(turn(x, -1, NX), y, z, c)
    up, down = device(x, y, turn(z, 1, NZ), c), device(x, y, turn(z, -1, NZ), c)
    other = device(x, y, z, 1 - c)
    enter(x, y, z, c)

    firsts = []
    for d in (1, 2, 3):
        firsts.append(links.send(own_ref, column.at[y], device(x, turn(y, d, NY), z, c)))
    weights = [links.send(kw_ref, kws_ref, other), links.send(vw_ref, vws_ref, other)]
    column[y] = own_ref[...]
    for copy in firsts:
        copy.wait_recv()
    half = own_ref.shape[-1]
    for p in range(CAP):
        for j in range(NY):
            rows[p, 4 * j : 4 * j + 4, :half] = column[j, p, 0:4, :]
            rows[p, 4 * j : 4 * j + 4, half:] = column[j, p, 4:8, :]
        held[p, x, z] = rows[p].astype(bf16)

    siblings, locals_ = [], []

    def keep(index):
        src = held.at[index]
        dst = all_ref.at[(c,) + index]
        siblings.append(links.send(src, dst, other))
        copy = pltpu.make_async_copy(src, dst, local_sem.at[len(locals_)])
        copy.start()
        locals_.append(copy)

    def ring(index, dev):
        return links.send(held.at[index], held.at[index], dev)

    both = pl.ds(0, 2)
    lo, hi = pl.ds(0, half), pl.ds(half, half)

    def x_start(zz):
        keep((both, x, zz))
        return zz, ring((both, x, zz), right), ring((both, x, zz), left)

    def x_next(state):
        zz, from_left, from_right = state
        from_left.wait_recv()
        a = ring((0, turn(x, -1, NX), zz), right)
        from_right.wait_recv()
        b = ring((1, turn(x, 1, NX), zz), left)
        keep((both, turn(x, -1, NX), zz))
        keep((both, turn(x, 1, NX), zz))
        return zz, a, b

    def x_end(state):
        zz, a, b = state
        a.wait_recv()
        b.wait_recv()
        keep((both, turn(x, 2, NX), zz))

    za = [(ring((both, x, z), up), ring((both, x, z), down))]
    xb = (ring((2, x, z), right), ring((2, x, z), left))
    stage1 = [[x_start(z)]]
    xb[0].wait_recv()
    xb2a = ring((2, turn(x, -1, NX), z, slice(None), lo), right)
    xb[1].wait_recv()
    xb2b = ring((2, turn(x, 1, NX), z, slice(None), hi), left)
    stage2 = []
    zb = None
    allx = slice(None)
    for s in (1, 2, 3, 4):
        below, above = turn(z, -s, NZ), turn(z, s, NZ)
        fa, fb = za[-1]
        fa.wait_recv()
        if s < 3:
            na = ring((both, x, below), up)
        elif s == 3:
            na = ring((0, x, below), up)
        fb.wait_recv()
        if s < 3:
            nb = ring((both, x, above), down)
        elif s == 3:
            nb = ring((1, x, above), down)
        if s < 4:
            za.append((na, nb))
            stage1.append([x_start(below), x_start(above)])
        else:
            stage1.append([x_start(below)])
        if s == 1:
            xb2a.wait_recv()
            xb2b.wait_recv()
            zb = (ring((2, allx, z), up), ring((2, allx, z), down))
            keep((2, allx, z))
        else:
            t = s - 1
            zb[0].wait_recv()
            na = ring((2, allx if t < 3 else pl.ds(0, 2), turn(z, -t, NZ)), up)
            zb[1].wait_recv()
            nb = ring((2, allx if t < 3 else pl.ds(2, 2), turn(z, t, NZ)), down)
            zb = (na, nb)
            keep((2, allx, turn(z, -t, NZ)))
            keep((2, allx, turn(z, t, NZ)))
        stage2.append([x_next(state) for state in stage1[s - 1]])
        if s >= 2:
            for state in stage2[s - 2]:
                x_end(state)
    stage2.append([x_next(state) for state in stage1[4]])
    for state in stage2[3] + stage2[4]:
        x_end(state)
    zb[0].wait_recv()
    zb[1].wait_recv()
    keep((2, allx, turn(z, 4, NZ)))

    for copy in weights + siblings:
        copy.wait_recv()
    for copy in locals_:
        copy.wait()
    links.finish()


def gather_latents(latents, key_weight, value_weight):
    width = latents.shape[2]
    stacked = latents.astype(f32).reshape(CAP, 4, 2, width // 2)
    stacked = stacked.transpose(0, 2, 1, 3).reshape(CAP, 8, width // 2)
    hbm = pl.BlockSpec(memory_space=pl.ANY)
    return pl.pallas_call(
        gather_kernel,
        name="gather_latents",
        out_shape=(
            jax.ShapeDtypeStruct((2, CAP, NX, NZ, 16, width), bf16),
            jax.ShapeDtypeStruct(key_weight.shape, bf16),
            jax.ShapeDtypeStruct(value_weight.shape, bf16),
        ),
        in_specs=[pl.BlockSpec(memory_space=pltpu.VMEM), hbm, hbm],
        out_specs=(hbm, hbm, hbm),
        scratch_shapes=[
            pltpu.VMEM((CAP, NX, NZ, 16, width), bf16),
            pltpu.VMEM((NY, CAP, 8, width // 2), f32),
            pltpu.VMEM((CAP, 16, width), f32),
            pltpu.SemaphoreType.DMA((GATHER_SEMS,)),
            pltpu.SemaphoreType.DMA((GATHER_SEMS,)),
            pltpu.SemaphoreType.DMA((64,)),
        ],
        compiler_params=pltpu.CompilerParams(
            collective_id=0, has_side_effects=True, vmem_limit_bytes=24 << 20
        ),
    )(stacked, key_weight, value_weight)


BLOCK = 128
GROUP = 8
CHUNK = 4


def attention_kernel(
    starts_ref, slot_ref, factor_ref, all_ref, q_ref, cot_ref, kw_ref, vw_ref,
    att_ref, gq_ref, gkv_ref, lat, keys, values, gacc, sem,
):
    images = slot_ref.shape[0]
    groups = images // GROUP
    group_rows = GROUP * 64
    tokens = q_ref.shape[0]
    heads = q_ref.shape[1] // HD
    hw = heads * HD
    scale = 1.0 / math.sqrt(HD)
    factor = factor_ref[0]

    def where_is(i):
        slot = slot_ref[i]
        enc = slot // CAP
        return slot - enc * CAP, lax.rem(enc, NX), enc // NX

    @pl.loop(0, images)
    def _(i):
        p, x, zh = where_is(i)
        for c in range(2):
            pltpu.make_async_copy(
                all_ref.at[c, p, x, pl.ds(2 * zh, 2)], lat.at[i, c], sem.at[i // GROUP]
            ).start()

    gkv_ref[...] = jnp.zeros_like(gkv_ref)
    for g in range(groups):
        rows = pl.ds(g * GROUP, GROUP)
        pltpu.make_async_copy(lat.at[rows], lat.at[rows], sem.at[g]).wait()
        data = lat[rows].reshape(group_rows, -1)
        out = pl.ds(g * group_rows, group_rows)
        keys[out, :] = jnp.dot(data, kw_ref[...], preferred_element_type=f32).astype(bf16)
        values[out, :] = jnp.dot(data, vw_ref[...], preferred_element_type=f32).astype(bf16)

    cols = CHUNK * 64
    nt = (((1,), (1,)), ((), ()))
    tn = (((0,), (0,)), ((), ()))

    @pl.loop(0, images // CHUNK)
    def _(q):
        edges = [starts_ref[q * CHUNK + j] for j in range(CHUNK + 1)]
        which = lax.broadcasted_iota(jnp.int32, (1, cols), 1) // 64
        first = jnp.full((1, cols), edges[0], jnp.int32)
        last = jnp.full((1, cols), edges[1], jnp.int32)
        for j in range(1, CHUNK):
            first = jnp.where(which == j, edges[j], first)
            last = jnp.where(which == j, edges[j + 1], last)
        krows = pl.ds(pl.multiple_of(q * cols, cols), cols)
        gacc[...] = jnp.zeros_like(gacc)

        @pl.loop(edges[0] // BLOCK, (edges[CHUNK] + BLOCK - 1) // BLOCK)
        def _(b):
            trows = pl.ds(pl.multiple_of(b * BLOCK, BLOCK), BLOCK)
            token = lax.broadcasted_iota(jnp.int32, (BLOCK, 1), 0) + b * BLOCK
            here = jnp.logical_and(token >= edges[0], token < edges[CHUNK])
            mask = jnp.logical_and(token >= first, token < last)
            for h in range(heads):
                hc = slice(h * HD, (h + 1) * HD)
                qb = q_ref[trows, hc]
                k = keys[krows, hc]
                v = values[krows, hc]
                gm = (factor * cot_ref[trows, hc].astype(f32)).astype(bf16)
                s = lax.dot_general(qb, k, nt, preferred_element_type=f32)
                gp = lax.dot_general(gm, v, nt, preferred_element_type=f32)
                s = jnp.where(mask, s * scale, -1e30)
                m = jnp.max(s, axis=1, keepdims=True)
                e = jnp.where(mask, jnp.exp(s - m), 0.0)
                total = jnp.sum(e, axis=1, keepdims=True)
                p = e * (1.0 / jnp.maximum(total, 1.0))
                pb = p.astype(bf16)
                w = jnp.sum(p * gp, axis=1, keepdims=True)
                gs = (p * (gp - w) * scale).astype(bf16)
                mix = jnp.dot(pb, v, preferred_element_type=f32)
                gq = jnp.dot(gs, k, preferred_element_type=f32)
                att_ref[trows, hc] = jnp.where(here, (factor * mix).astype(bf16), att_ref[trows, hc])
                gq_ref[trows, hc] = jnp.where(here, gq.astype(bf16), gq_ref[trows, hc])
                gacc[:, hc] += lax.dot_general(gs, qb, tn, preferred_element_type=f32)
                vc = slice(hw + h * HD, hw + (h + 1) * HD)
                gacc[:, vc] += lax.dot_general(pb, gm, tn, preferred_element_type=f32)

        for j in range(CHUNK):
            p, x, zh = where_is(q * CHUNK + j)
            for c in range(2):
                r = j * 64 + c * 32
                gkv_ref[c, p, x, pl.ds(2 * zh, 2)] = (
                    gacc[r : r + 32, :].astype(bf16).reshape(2, 16, 2 * hw)
                )


def attention(starts, image_slot, factor, everyone, queries, cotangent, key_weight, value_weight):
    tokens, hw = queries.shape
    width = key_weight.shape[0]
    images = image_slot.shape[0]
    vmem = pl.BlockSpec(memory_space=pltpu.VMEM)
    smem = pl.BlockSpec(memory_space=pltpu.SMEM)
    hbm = pl.BlockSpec(memory_space=pl.ANY)
    return pl.pallas_call(
        attention_kernel,
        name="attention",
        out_shape=(
            jax.ShapeDtypeStruct((tokens, hw), bf16),
            jax.ShapeDtypeStruct((tokens, hw), bf16),
            jax.ShapeDtypeStruct((2, CAP, NX, NZ, 16, 2 * hw), bf16),
        ),
        in_specs=[smem, smem, smem, hbm, vmem, vmem, vmem, vmem],
        out_specs=(vmem, vmem, vmem),
        scratch_shapes=[
            pltpu.VMEM((images, 2, 2, 16, width), bf16),
            pltpu.VMEM((images * 64, hw), bf16),
            pltpu.VMEM((images * 64, hw), bf16),
            pltpu.VMEM((CHUNK * 64, 2 * hw), f32),
            pltpu.SemaphoreType.DMA((images // GROUP,)),
        ],
        compiler_params=pltpu.CompilerParams(vmem_limit_bytes=40 << 20),
    )(starts, image_slot, factor, everyone, queries, cotangent, key_weight, value_weight)


SCATTER_SEMS = 80


def scatter_kernel(
    gkv_ref, kw_ref, vw_ref, kws_ref, vws_ref, out_ref,
    mine, theirs, part, xin, zin, xb_in, zb_in, col_out, col_in, total, send_sem, recv_sem, local_sem,
):
    x, y, z, c = place()
    links = Links(send_sem, recv_sem)
    right, left = device(turn(x, 1, NX), y, z, c), device(turn(x, -1, NX), y, z, c)
    up, down = device(x, y, turn(z, 1, NZ), c), device(x, y, turn(z, -1, NZ), c)
    other = device(x, y, z, 1 - c)
    hw = kw_ref.shape[1]
    width = kw_ref.shape[0]
    half = width // 2
    nt = (((1,), (1,)), ((), ()))
    enter(x, y, z, c)

    own = pltpu.make_async_copy(gkv_ref.at[c], mine, local_sem.at[0])
    own.start()
    pieces = []
    for k in (2, 1, -1, 0):
        xx = turn(x, k, NX)
        pieces.append(
            links.send(gkv_ref.at[1 - c, pl.ds(0, 2), xx], theirs.at[pl.ds(0, 2), xx], other)
        )
    piece_b = links.send(gkv_ref.at[1 - c, 2], theirs.at[2], other)
    own.wait()

    def project(a, b):
        r = lax.dot_general(a[:, :hw], kw_ref[...], nt, preferred_element_type=f32)
        r += lax.dot_general(a[:, hw:], vw_ref[...], nt, preferred_element_type=f32)
        r += lax.dot_general(b[:, :hw], kws_ref[...], nt, preferred_element_type=f32)
        r += lax.dot_general(b[:, hw:], vws_ref[...], nt, preferred_element_type=f32)
        return r.astype(bf16)

    def compute_a(i, k):
        pieces[i].wait_recv()
        xx = turn(x, k, NX)
        for p in range(2):
            a = mine[p, xx].reshape(NZ * 16, 2 * hw)
            b = theirs[p, xx].reshape(NZ * 16, 2 * hw)
            part[p, xx] = project(a, b).reshape(NZ, 16, width)

    def compute_b(xx):
        a = mine[2, xx].reshape(NZ * 16, 2 * hw)
        b = theirs[2, xx].reshape(NZ * 16, 2 * hw)
        part[2, xx] = project(a, b).reshape(NZ, 16, width)

    def plus(index, arrived):
        part[index] = (part[index].astype(f32) + arrived.astype(f32)).astype(bf16)

    compute_a(0, 2)
    far = turn(x, 2, NX)
    a1 = links.send(part.at[0, far], xin.at[0], right)
    b1 = links.send(part.at[1, far], xin.at[1], left)
    piece_b.wait_recv()
    for xx in range(NX):
        compute_b(xx)
    zf = turn(z, 4, NZ)
    zb = [
        links.send(part.at[2, pl.ds(0, 2), zf], zb_in.at[0, 0, pl.ds(0, 2)], up),
        links.send(part.at[2, pl.ds(2, 2), zf], zb_in.at[1, 0, pl.ds(2, 2)], down),
    ]
    compute_a(1, 1)
    compute_a(2, -1)
    xr, xl = turn(x, 1, NX), turn(x, -1, NX)
    a2 = links.send(part.at[1, xr], xin.at[2], right)
    b2 = links.send(part.at[0, xl], xin.at[3], left)
    compute_a(3, 0)

    def zb_step(s, zb):
        k = 4 - s
        zr, zl = turn(z, k, NZ), turn(z, -k, NZ)
        zb[0].wait_recv()
        if s == 1:
            for xx in (0, 1):
                plus((2, xx, zr), zb_in[0, 0, xx])
        else:
            for xx in range(NX):
                plus((2, xx, zr), zb_in[0, s - 1, xx])
        if k:
            n0 = links.send(part.at[2, :, zr], zb_in.at[0, s], up)
        zb[1].wait_recv()
        if s == 1:
            for xx in (2, 3):
                plus((2, xx, zl), zb_in[1, 0, xx])
        else:
            for xx in range(NX):
                plus((2, xx, zl), zb_in[1, s - 1, xx])
        if k:
            n1 = links.send(part.at[2, :, zl], zb_in.at[1, s], down)
            return [n0, n1]

    zb = zb_step(1, zb)
    a1.wait_recv()
    for zz in range(NZ):
        plus((0, xr, zz), xin[0, zz])
    a3 = links.send(part.at[0, xr], xin.at[4], right)
    b1.wait_recv()
    for zz in range(NZ):
        plus((1, xl, zz), xin[1, zz])
    b3 = links.send(part.at[1, xl], xin.at[5], left)
    zb = zb_step(2, zb)
    zb = zb_step(3, zb)
    a2.wait_recv()
    b2.wait_recv()
    for zz in range(NZ):
        plus((1, x, zz), xin[2, zz])
        plus((0, x, zz), xin[3, zz])
    zb_step(4, zb)
    xf = turn(x, 2, NX)
    c1 = links.send(part.at[2, xf, z, :, pl.ds(0, half)], xb_in.at[0], right)
    d1 = links.send(part.at[2, xf, z, :, pl.ds(half, half)], xb_in.at[1], left)
    c2 = links.send(part.at[2, xr, z, :, pl.ds(half, half)], xb_in.at[2], right)
    d2 = links.send(part.at[2, xl, z, :, pl.ds(0, half)], xb_in.at[3], left)
    a3.wait_recv()
    b3.wait_recv()
    for zz in range(NZ):
        plus((0, x, zz), xin[4, zz])
        plus((1, x, zz), xin[5, zz])
    za = [
        links.send(part.at[0, x, zf], zin.at[0, 0, 0], up),
        links.send(part.at[1, x, zf], zin.at[1, 0, 1], down),
    ]
    c1.wait_recv()
    cols = pl.ds(0, half)
    part[2, xr, z, :, cols] = (part[2, xr, z, :, cols].astype(f32) + xb_in[0].astype(f32)).astype(bf16)
    c3 = links.send(part.at[2, xr, z, :, pl.ds(0, half)], xb_in.at[4], right)
    d1.wait_recv()
    cols = pl.ds(half, half)
    part[2, xl, z, :, cols] = (part[2, xl, z, :, cols].astype(f32) + xb_in[1].astype(f32)).astype(bf16)
    d3 = links.send(part.at[2, xl, z, :, pl.ds(half, half)], xb_in.at[5], left)
    for s in (1, 2, 3):
        k = 4 - s
        zr, zl = turn(z, k, NZ), turn(z, -k, NZ)
        za[0].wait_recv()
        for p in (0,) if s == 1 else (0, 1):
            plus((p, x, zr), zin[0, s - 1, p])
        n0 = links.send(part.at[pl.ds(0, 2), x, zr], zin.at[0, s], up)
        za[1].wait_recv()
        for p in (1,) if s == 1 else (0, 1):
            plus((p, x, zl), zin[1, s - 1, p])
        n1 = links.send(part.at[pl.ds(0, 2), x, zl], zin.at[1, s], down)
        za = [n0, n1]
    za[0].wait_recv()
    za[1].wait_recv()
    for p in range(2):
        total[p] = part[p, x, z].astype(f32) + zin[0, 3, p].astype(f32) + zin[1, 3, p].astype(f32)
    for copy in (c2, d2, c3, d3):
        copy.wait_recv()
    last = part[2, x, z].astype(f32)
    total[2, :, :half] = last[:, :half] + xb_in[3].astype(f32) + xb_in[4].astype(f32)
    total[2, :, half:] = last[:, half:] + xb_in[2].astype(f32) + xb_in[5].astype(f32)

    for j in range(NY):
        for p in range(CAP):
            col_out[j, p, 0:4, :] = total[p, 4 * j : 4 * j + 4, :half]
            col_out[j, p, 4:8, :] = total[p, 4 * j : 4 * j + 4, half:]
    ends = []
    for d in (1, 2, 3):
        yy = turn(y, d, NY)
        ends.append(links.send(col_out.at[yy], col_in.at[d - 1], device(x, yy, z, c)))
    result = col_out[y]
    for d in range(3):
        ends[d].wait_recv()
        result = result + col_in[d]
    out_ref[...] = result
    links.finish()


def scatter_latents(gkv, kw, vw, kws, vws):
    width, hw = kw.shape
    half = width // 2
    vmem = pl.BlockSpec(memory_space=pltpu.VMEM)
    hbm = pl.BlockSpec(memory_space=pl.ANY)
    out = pl.pallas_call(
        scatter_kernel,
        name="scatter_latents",
        out_shape=jax.ShapeDtypeStruct((CAP, 8, half), f32),
        in_specs=[hbm, vmem, vmem, vmem, vmem],
        out_specs=vmem,
        scratch_shapes=[
            pltpu.VMEM((CAP, NX, NZ, 16, 2 * hw), bf16),
            pltpu.VMEM((CAP, NX, NZ, 16, 2 * hw), bf16),
            pltpu.VMEM((CAP, NX, NZ, 16, width), bf16),
            pltpu.VMEM((6, NZ, 16, width), bf16),
            pltpu.VMEM((2, 4, 2, 16, width), bf16),
            pltpu.VMEM((6, 16, half), bf16),
            pltpu.VMEM((2, 4, NX, 16, width), bf16),
            pltpu.VMEM((NY, CAP, 8, half), f32),
            pltpu.VMEM((NY - 1, CAP, 8, half), f32),
            pltpu.VMEM((CAP, 16, width), f32),
            pltpu.SemaphoreType.DMA((SCATTER_SEMS,)),
            pltpu.SemaphoreType.DMA((SCATTER_SEMS,)),
            pltpu.SemaphoreType.DMA((1,)),
        ],
        compiler_params=pltpu.CompilerParams(
            collective_id=1, has_side_effects=True, vmem_limit_bytes=48 << 20
        ),
    )(gkv, kw, vw, kws, vws)
    return out.reshape(CAP, 2, 4, half).transpose(0, 2, 1, 3).reshape(CAP, 4, width)


def image_slots(image_counts, images):
    image_ends = jnp.cumsum(image_counts)
    image_starts = image_ends - image_counts
    index = jnp.arange(images, dtype=jnp.int32)
    owner = jnp.sum((index[:, None] >= image_ends[None, :]).astype(jnp.int32), axis=1)
    match = owner[:, None] == jnp.arange(image_counts.shape[0], dtype=jnp.int32)[None, :]
    first = jnp.sum(jnp.where(match, image_starts[None, :], 0), axis=1)
    return owner * CAP + index - first


def on_device(
    latents, key_weight, value_weight, gate_logit, queries, cotangent, image_counts, token_image
):
    images = 2 * image_counts.shape[0]
    kw, vw = key_weight[0], value_weight[0]
    image_slot = image_slots(image_counts, images).astype(jnp.int32)
    edge = jnp.arange(images + 1, dtype=jnp.int32)
    starts = jnp.sum((token_image[None, :] < edge[:, None]).astype(jnp.int32), axis=1)
    factor = jnp.tanh(gate_logit)
    everyone, kws, vws = gather_latents(latents, kw, vw)
    attended, grad_queries, gkv = attention(
        starts, image_slot, factor, everyone, queries[0], cotangent[0], kw, vw
    )
    grad_latents = scatter_latents(gkv, kw, vw, kws, vws)
    return attended[None], grad_queries[None], grad_latents


def solution(mesh):
    shards = P("section", None, "enc")
    return jax.shard_map(
        on_device,
        mesh=mesh,
        in_specs=(
            P("enc", "section", None), shards, shards, P("section"), shards, shards, P(), P(),
        ),
        out_specs=(shards, shards, P("enc", "section", None)),
        check_vma=False,
    )
```

```python
import math

import jax
import jax.numpy as jnp
from jax import lax
from jax.experimental import pallas as pl
from jax.experimental.pallas import tpu as pltpu
from jax.sharding import PartitionSpec as P

HD = 128
CAP = 3
NX, NY, NZ = 4, 4, 8
MESH = pl.DeviceIdType.MESH
f32 = jnp.float32
bf16 = jnp.bfloat16


def place():
    section = lax.axis_index("section")
    enc = lax.axis_index("enc")
    x = lax.rem(enc, NX)
    y = lax.rem(section // 2, NY)
    z = (enc // NX) * 2 + section // (2 * NY)
    return x, y, z, lax.rem(section, 2)


def device(x, y, z, c):
    return (lax.rem(z, 2) * (2 * NY) + y * 2 + c, (z // 2) * NX + x)


def turn(a, d, n):
    return lax.rem(a + d + n, n)


class Links:
    def __init__(self, send_sem, recv_sem):
        self.send_sem, self.recv_sem = send_sem, recv_sem
        self.used = 0
        self.sent = []

    def send(self, src, dst, dev):
        i = self.used
        self.used += 1
        copy = pltpu.make_async_remote_copy(
            src_ref=src,
            dst_ref=dst,
            send_sem=self.send_sem.at[i],
            recv_sem=self.recv_sem.at[i],
            device_id=dev,
            device_id_type=MESH,
        )
        copy.start()
        self.sent.append(copy)
        return copy

    def finish(self):
        for copy in self.sent:
            copy.wait_send()


def greet(x, y, z, c):
    peers = [device(x, turn(y, d, NY), z, c) for d in (1, 2, 3)]
    peers += [device(turn(x, d, NX), y, z, c) for d in (1, 2, 3)]
    peers += [device(x, y, turn(z, d, NZ), c) for d in (1, -1, 2, -2)]
    peers += [device(x, y, z, 1 - c)]
    barrier = pltpu.get_barrier_semaphore()
    for peer in peers:
        pl.semaphore_signal(barrier, inc=1, device_id=peer, device_id_type=MESH)


def meet():
    pl.semaphore_wait(pltpu.get_barrier_semaphore(), NX + NY + 3)


GATHER_SEMS = 160
XCUT, YCUT = 640, 1152
QUARTER = (YCUT - XCUT) // NY


def gather_kernel(
    own_hbm, kw_ref, vw_ref, kv_ref, kws_ref, vws_ref,
    hx, hy, hz, own, mine, column, rows, kw, vw, kv, send_sem, recv_sem, local_sem,
):
    x, y, z, c = place()
    links = Links(send_sem, recv_sem)
    right, left = device(turn(x, 1, NX), y, z, c), device(turn(x, -1, NX), y, z, c)
    north, south = device(x, turn(y, 1, NY), z, c), device(x, turn(y, -1, NY), z, c)
    along = {d: device(x, y, turn(z, d, NZ), c) for d in (-2, -1, 1, 2)}
    other = device(x, y, z, 1 - c)
    width = own_hbm.shape[-1]
    hw = kw_ref.shape[-1]
    greet(x, y, z, c)
    first = pltpu.make_async_copy(own_hbm, own, local_sem.at[2])
    first.start()
    loads = [
        pltpu.make_async_copy(kw_ref, kw, local_sem.at[0]),
        pltpu.make_async_copy(vw_ref, vw, local_sem.at[1]),
    ]
    for copy in loads:
        copy.start()
    first.wait()
    for p in range(CAP):
        mine[4 * p : 4 * p + 4, :] = own[p].astype(f32)
    mine[12:16, :] = jnp.zeros((4, width), f32)
    column[y] = mine[...].astype(bf16)
    meet()

    firsts = []
    for d in (1, 3, 2):
        firsts.append(links.send(column.at[y], column.at[y], device(x, turn(y, d, NY), z, c)))

    for copy in firsts:
        copy.wait_recv()
    for j in range(NY):
        block = column[j].astype(f32)
        for p in range(CAP):
            rows[p, 4 * j : 4 * j + 4, :] = block[4 * p : 4 * p + 4, :]
    part = pl.ds(pl.multiple_of(XCUT + y * QUARTER, 128), QUARTER)
    hx[c, z, x] = rows[:, :, :XCUT].astype(bf16)
    hy[c, z, y, x] = rows[:, :, part].astype(bf16)
    hz[c, z, x] = rows[:, :, YCUT:].astype(bf16)

    def send(ref, dev):
        return links.send(ref, ref, dev)

    def arrive(*copies):
        for copy in copies:
            copy.wait_recv()

    stores = []

    def project(zz):
        n = 2 * NX * CAP * 16
        data = [hx[:, zz].reshape(n, XCUT)]
        data += [hy[:, zz, j].reshape(n, QUARTER) for j in range(NY)]
        data += [hz[:, zz].reshape(n, width - YCUT)]
        data = jnp.concatenate(data, axis=1)
        for w, cols in ((kw, slice(0, hw)), (vw, slice(hw, 2 * hw))):
            r = jnp.dot(data, w[...], preferred_element_type=f32).astype(bf16)
            kv[:, zz, :, :, :, cols] = r.reshape(2, NX, CAP, 16, hw)
        copy = pltpu.make_async_copy(kv.at[:, zz], kv_ref.at[:, zz], local_sem.at[3 + len(stores)])
        copy.start()
        stores.append(copy)

    x1, x3 = turn(x, 1, NX), turn(x, -1, NX)
    y1, y3 = turn(y, 1, NY), turn(y, -1, NY)
    xpeers = [device(turn(x, d, NX), y, z, c) for d in (1, 3, 2)]
    few, many = pl.ds(0, 1), pl.ds(1, 2)
    front, back = pl.ds(0, 2), pl.ds(2, 2)

    class Last:
        def __init__(self, axis, k):
            self.axis, self.k, self.zz = axis, k, turn(z, k, NZ)
            if axis == 0:
                self.go = [send(hx.at[c, self.zz, x], dev) for dev in (right, left)]
            else:
                self.go = [send(hy.at[c, self.zz, y], dev) for dev in (north, south)]

        def forward(self):
            a, b = self.go
            if self.axis == 0:
                sa, sb = (few, many) if self.k % 2 else (many, few)
                arrive(a)
                a = send(hx.at[c, self.zz, x3, sa], right)
                arrive(b)
                b = send(hx.at[c, self.zz, x1, sb], left)
            else:
                arrive(a)
                a = send(hy.at[c, self.zz, y3, front], north)
                arrive(b)
                b = send(hy.at[c, self.zz, y1, back], south)
            self.go = [a, b]

        def end(self):
            arrive(*self.go)
            self.kept = send((hx if self.axis == 0 else hy).at[c, self.zz], other)

    def block(axis, k, cut=None):
        zz = turn(z, k, NZ)
        ref = hx.at[c, zz, x] if axis == 0 else hy.at[c, zz, y]
        return ref if cut is None else ref.at[cut]

    def over_z(axis):
        return {d: send(block(axis, 0), along[d]) for d in (1, -1, 2, -2)}

    def over_z_again(axis, go):
        go2 = {}
        cut = (few, many) if axis == 0 else (pl.ds(0, 3), pl.ds(3, 1))
        for d, s in ((2, 0), (-2, 1)):
            arrive(go[d])
            go2[3 * d // 2] = send(block(axis, -d), along[d // 2])
            go2[2 * d] = send(block(axis, -d, cut[s]), along[d])
        return go2

    y_first = [send(hy.at[c, z, y, x], dev) for dev in xpeers]
    go_x = over_z(0)
    z_first = [send(hz.at[c, z, x], dev) for dev in xpeers]
    last = {(0, 0): Last(0, 0)}
    arrive(*y_first)
    go_y = over_z(1)
    last[1, 0] = Last(1, 0)
    arrive(*z_first)
    go_z = [send(hz.at[c, z], along[1]), send(hz.at[c, z], along[-1])]
    zkept = {0: send(hz.at[c, z], other)}
    weights = [links.send(kw_ref, kws_ref, other), links.send(vw_ref, vws_ref, other)]

    def ring_z(s):
        out = []
        for i, d in ((0, -s), (1, s)):
            zz = turn(z, d, NZ)
            arrive(go_z[i])
            if s < 3:
                out.append(send(hz.at[c, zz], along[1 - 2 * i]))
            elif s == 3:
                out.append(send(hz.at[c, zz, (front, back)[i]], along[1 - 2 * i]))
            if s < 4 or i:
                zkept[d] = send(hz.at[c, zz], other)
        return out

    def finish(k):
        arrive(last[0, k].kept, last[1, k].kept, zkept[k])
        project(turn(z, k, NZ))

    for copy in loads:
        copy.wait()
    for d in (1, -1):
        arrive(go_x[d])
        last[0, -d] = Last(0, -d)
    far_x = over_z_again(0, go_x)
    for d in (2, -2):
        last[0, d] = Last(0, d)
    last[0, 0].forward()
    for d in (1, -1):
        arrive(go_y[d])
        last[1, -d] = Last(1, -d)
    far_y = over_z_again(1, go_y)
    for d in (2, -2):
        last[1, d] = Last(1, d)
    last[1, 0].forward()
    go_z = ring_z(1)
    for d in (1, -1):
        last[0, d].forward()
    for d in (3, -3):
        arrive(far_x[d])
        last[0, -d] = Last(0, -d)
    arrive(far_x[4], far_x[-4])
    last[0, 4] = Last(0, 4)
    for d in (1, -1):
        last[1, d].forward()
    for d in (3, -3):
        arrive(far_y[d])
        last[1, -d] = Last(1, -d)
    arrive(far_y[4], far_y[-4])
    last[1, 4] = Last(1, 4)
    go_z = ring_z(2)
    last[0, 0].end()
    last[1, 0].end()
    for d in (2, -2):
        last[0, d].forward()
        last[1, d].forward()
    for d in (1, -1):
        last[0, d].end()
        last[1, d].end()
    finish(0)
    go_z = ring_z(3)
    for d in (3, -3):
        last[0, d].forward()
        last[1, d].forward()
    last[0, 4].forward()
    last[1, 4].forward()
    for d in (2, -2):
        last[0, d].end()
        last[1, d].end()
    finish(1)
    finish(-1)
    ring_z(4)
    for d in (3, -3):
        last[0, d].end()
        last[1, d].end()
    finish(2)
    finish(-2)
    last[0, 4].end()
    last[1, 4].end()
    finish(3)
    finish(-3)
    finish(4)

    arrive(*weights)
    for copy in stores:
        copy.wait()
    links.finish()


def gather_latents(latents, key_weight, value_weight):
    width = latents.shape[2]
    hw = key_weight.shape[1]
    hbm = pl.BlockSpec(memory_space=pltpu.HBM)
    return pl.pallas_call(
        gather_kernel,
        name="gather_latents",
        out_shape=(
            jax.ShapeDtypeStruct((2, NZ, NX, CAP, 16, 2 * hw), bf16),
            jax.ShapeDtypeStruct(key_weight.shape, bf16),
            jax.ShapeDtypeStruct(value_weight.shape, bf16),
        ),
        in_specs=[hbm, hbm, hbm],
        out_specs=(hbm, hbm, hbm),
        scratch_shapes=[
            pltpu.VMEM((2, NZ, NX, CAP, 16, XCUT), bf16),
            pltpu.VMEM((2, NZ, NY, NX, CAP, 16, QUARTER), bf16),
            pltpu.VMEM((2, NZ, NX, CAP, 16, width - YCUT), bf16),
            pltpu.VMEM(latents.shape, bf16),
            pltpu.VMEM((16, width), f32),
            pltpu.VMEM((NY, 16, width), bf16),
            pltpu.VMEM((CAP, 16, width), f32),
            pltpu.VMEM(key_weight.shape, bf16),
            pltpu.VMEM(value_weight.shape, bf16),
            pltpu.VMEM((2, NZ, NX, CAP, 16, 2 * hw), bf16),
            pltpu.SemaphoreType.DMA((GATHER_SEMS,)),
            pltpu.SemaphoreType.DMA((GATHER_SEMS,)),
            pltpu.SemaphoreType.DMA((12,)),
        ],
        compiler_params=pltpu.CompilerParams(
            collective_id=0, has_side_effects=True, vmem_limit_bytes=62 << 20
        ),
    )(latents, key_weight, value_weight)


BLOCK = 128
CHUNK = 4
SIDE = 4


def attention_kernel(
    counts_ref, gate_ref, token_ref, kv_ref, q_hbm, cot_hbm,
    att_hbm, gq_hbm, gkv_ref,
    kvs, stage, zeros, q_ref, cot_ref, att_ref, gq_ref, gacc,
    slots, starts, chunk_of, block_of, begin_of, sem, io_sem,
):
    owners = counts_ref.shape[0]
    images = 2 * owners
    chunks = images // CHUNK
    heads = q_ref.shape[1] // HD
    hw = heads * HD
    scale = 1.0 / math.sqrt(HD)
    cols = CHUNK * 64
    tokens = q_ref.shape[0]
    pairs = chunk_of.shape[0]
    nt = (((1,), (1,)), ((), ()))

    copies = [
        pltpu.make_async_copy(q_hbm, q_ref, io_sem.at[0]),
        pltpu.make_async_copy(cot_hbm, cot_ref, io_sem.at[1]),
        pltpu.make_async_copy(att_ref, att_hbm, io_sem.at[4]),
        pltpu.make_async_copy(gq_ref, gq_hbm, io_sem.at[5]),
    ]
    zeros[...] = jnp.zeros_like(zeros)
    n = 0
    for e in range(owners):
        count = counts_ref[e]
        x, zs = e % NX, pl.ds(2 * (e // NX), 2)
        for p in range(CAP):

            @pl.when(p < count)
            def _():
                slots[n + p] = e * CAP + p
                for c in range(2):
                    pltpu.make_async_copy(
                        kv_ref.at[c, zs, x, p], kvs.at[n + p, c], sem.at[0]
                    ).start()

            @pl.when(p >= count)
            def _():
                for c in range(2):
                    pltpu.make_async_copy(zeros, gkv_ref.at[c, zs, x, p], io_sem.at[2]).start()

        n = n + count
        if e == 1:
            copies[0].start()
            copies[1].start()
    token_image = token_ref[...]
    for i in range(images + 1):
        starts[i] = jnp.sum((token_image < i).astype(jnp.int32))
    factor = jnp.tanh(jnp.full((1, HD), gate_ref[0], f32))
    for i in range(pairs):
        chunk_of[i] = 0
        block_of[i] = 0
        begin_of[i] = tokens
    n = 0
    for q in range(chunks):
        b0 = starts[q * CHUNK] // BLOCK
        b1 = (starts[(q + 1) * CHUNK] + BLOCK - 1) // BLOCK

        @pl.loop(b0, b1)
        def _(b):
            i = n + b - b0
            chunk_of[i] = q
            block_of[i] = b
            begin_of[i] = b * BLOCK

        n = n + b1 - b0
    gacc[...] = jnp.zeros_like(gacc)
    copies[0].wait()
    copies[1].wait()
    pltpu.make_async_copy(kvs, kvs, sem.at[0]).wait()

    @pl.loop(0, (n + SIDE - 1) // SIDE)
    def _(step):
        work = []
        for u in range(SIDE):
            i = step * SIDE + u
            q, b, begin = chunk_of[i], block_of[i], begin_of[i]
            four = pl.ds(q * CHUNK, CHUNK)
            trows = pl.ds(pl.multiple_of(b * BLOCK, BLOCK), BLOCK)
            krows = pl.ds(pl.multiple_of(q * cols, cols), cols)
            edges = [starts[q * CHUNK + j] for j in range(CHUNK + 1)]
            which = lax.broadcasted_iota(jnp.int32, (1, cols), 1) // 64
            first = jnp.full((1, cols), edges[0], jnp.int32)
            last = jnp.full((1, cols), edges[1], jnp.int32)
            for j in range(1, CHUNK):
                first = jnp.where(which == j, edges[j], first)
                last = jnp.where(which == j, edges[j + 1], last)
            token = lax.broadcasted_iota(jnp.int32, (BLOCK, 1), 0) + begin
            here = jnp.logical_and(token >= edges[0], token < edges[CHUNK])
            wide = jnp.logical_and(token >= first, token < last).astype(f32).astype(bf16)
            lane = lax.broadcasted_iota(jnp.int32, (1, BLOCK), 1) + begin
            tall = [
                jnp.logical_and(lane >= edges[j], lane < edges[j + 1]) for j in range(CHUNK)
            ]
            ones = [t.astype(f32).astype(bf16) for t in tall]
            for h in range(heads):
                hc = slice(h * HD, (h + 1) * HD)
                vc = slice(hw + h * HD, hw + (h + 1) * HD)
                qb = q_ref[trows, hc]
                k = kvs[four, :, :, :, hc].reshape(cols, HD)
                v = kvs[four, :, :, :, vc].reshape(cols, HD)
                gm = (factor * cot_ref[trows, hc].astype(f32)).astype(bf16)
                s = lax.dot_general(k, qb, nt, preferred_element_type=f32)
                gp = lax.dot_general(v, gm, nt, preferred_element_type=f32)
                work.append((hc, vc, trows, krows, here, wide, tall, ones, qb, k, v, gm, s, gp))

        def pick(full, tall):
            out = full[(CHUNK - 1) * 64 :]
            for j in range(CHUNK - 1):
                out = jnp.where(tall[j], full[j * 64 : (j + 1) * 64], out)
            return out

        def spread(small, ones, wide):
            rows = small.astype(bf16)
            down = jnp.concatenate([rows * ones[j] for j in range(CHUNK)], axis=0)
            twice = jnp.concatenate([small, small], axis=0).T.astype(bf16)
            return down, jnp.concatenate([twice] * (CHUNK // 2), axis=1) * wide

        done = []
        for hc, vc, trows, krows, here, wide, tall, ones, qb, k, v, gm, s, gp in work:
            s = pick(s, tall)
            gp = pick(gp, tall)
            e = jnp.exp((s - jnp.max(s, axis=0, keepdims=True)) * scale)
            p = e * (1.0 / jnp.sum(e, axis=0, keepdims=True))
            w = jnp.sum(p * gp, axis=0, keepdims=True)
            gs = p * (gp - w) * scale
            p_down, p_wide = spread(p, ones, wide)
            gs_down, gs_wide = spread(gs, ones, wide)
            done.append((
                jnp.dot(p_wide, v, preferred_element_type=f32),
                jnp.dot(gs_wide, k, preferred_element_type=f32),
                jnp.dot(gs_down, qb, preferred_element_type=f32),
                jnp.dot(p_down, gm, preferred_element_type=f32),
            ))
        for item, (mix, gq, gk, gv) in zip(work, done):
            hc, vc, trows, krows, here = item[:5]
            att_ref[trows, hc] = jnp.where(here, (factor * mix).astype(bf16), att_ref[trows, hc])
            gq_ref[trows, hc] = jnp.where(here, gq.astype(bf16), gq_ref[trows, hc])
            gacc[krows, hc] += gk
            gacc[krows, vc] += gv

    copies[2].start()
    copies[3].start()

    @pl.loop(0, chunks)
    def _(q):
        krows = pl.ds(pl.multiple_of(q * cols, cols), cols)
        stage[pl.ds(q * CHUNK, CHUNK)] = (
            gacc[krows, :].astype(bf16).reshape(CHUNK, 2, 2, 16, 2 * hw)
        )
        for j in range(CHUNK):
            i = q * CHUNK + j
            slot = slots[i]
            enc = slot // CAP
            for c in range(2):
                pltpu.make_async_copy(
                    stage.at[i, c],
                    gkv_ref.at[c, pl.ds(2 * (enc // NX), 2), lax.rem(enc, NX), slot - enc * CAP],
                    io_sem.at[3],
                ).start()

    empty = stage.at[pl.ds(0, CAP * owners - images)]
    pltpu.make_async_copy(empty, empty, io_sem.at[2]).wait()
    pltpu.make_async_copy(stage, stage, io_sem.at[3]).wait()
    copies[2].wait()
    copies[3].wait()


def attention(image_counts, gate_logit, token_image, kv, queries, cotangent):
    tokens, hw = queries.shape
    images = 2 * image_counts.shape[0]
    pairs = images // CHUNK + tokens // BLOCK
    vmem = pl.BlockSpec(memory_space=pltpu.VMEM)
    smem = pl.BlockSpec(memory_space=pltpu.SMEM)
    hbm = pl.BlockSpec(memory_space=pltpu.HBM)
    return pl.pallas_call(
        attention_kernel,
        name="attention",
        out_shape=(
            jax.ShapeDtypeStruct((tokens, hw), bf16),
            jax.ShapeDtypeStruct((tokens, hw), bf16),
            jax.ShapeDtypeStruct((2, NZ, NX, CAP, 16, 2 * hw), bf16),
        ),
        in_specs=[smem, smem, vmem, hbm, hbm, hbm],
        out_specs=(hbm, hbm, hbm),
        scratch_shapes=[
            pltpu.VMEM((images, 2, 2, 16, 2 * hw), bf16),
            pltpu.VMEM((images, 2, 2, 16, 2 * hw), bf16),
            pltpu.VMEM((2, 16, 2 * hw), bf16),
            pltpu.VMEM((tokens, hw), bf16),
            pltpu.VMEM((tokens, hw), bf16),
            pltpu.VMEM((tokens, hw), bf16),
            pltpu.VMEM((tokens, hw), bf16),
            pltpu.VMEM((images * 64, 2 * hw), f32),
            pltpu.SMEM((images,), jnp.int32),
            pltpu.SMEM((images + 1,), jnp.int32),
            pltpu.SMEM((pairs,), jnp.int32),
            pltpu.SMEM((pairs,), jnp.int32),
            pltpu.SMEM((pairs,), jnp.int32),
            pltpu.SemaphoreType.DMA((1,)),
            pltpu.SemaphoreType.DMA((6,)),
        ],
        compiler_params=pltpu.CompilerParams(vmem_limit_bytes=62 << 20),
    )(image_counts, gate_logit, token_image.reshape(8, tokens // 8), kv, queries, cotangent)


SCATTER_SEMS = 128


def scatter_kernel(
    gkv_ref, kw_hbm, vw_hbm, kws_hbm, vws_hbm, out_ref,
    weights, mine, theirs, px, py, pz, rx1, rx2, ry1, ry2, zx, zx4, zy, zy4, rz, ty, tz, ly, lz,
    total, col, col_out, col_in, send_sem, recv_sem, local_sem,
):
    x, y, z, c = place()
    links = Links(send_sem, recv_sem)
    right, left = device(turn(x, 1, NX), y, z, c), device(turn(x, -1, NX), y, z, c)
    north, south = device(x, turn(y, 1, NY), z, c), device(x, turn(y, -1, NY), z, c)
    along = {d: device(x, y, turn(z, d, NZ), c) for d in (-2, -1, 1, 2)}
    other = device(x, y, z, 1 - c)
    hw = kw_hbm.shape[1]
    width = kw_hbm.shape[0]
    rest = width - YCUT
    nt = (((1,), (1,)), ((), ()))
    greet(x, y, z, c)
    loads = [pltpu.make_async_copy(gkv_ref.at[c], mine, local_sem.at[0])]
    for i, ref in enumerate((kw_hbm, vw_hbm, kws_hbm, vws_hbm)):
        loads.append(pltpu.make_async_copy(ref, weights.at[i], local_sem.at[1 + i]))
    for copy in loads:
        copy.start()
    meet()
    order = (4, 3, -3, 2, -2, 1, -1, 0)
    at = {k: turn(z, k, NZ) for k in order}
    pieces = {k: links.send(gkv_ref.at[1 - c, at[k]], theirs.at[at[k]], other) for k in order}
    for copy in loads:
        copy.wait()

    def arrive(*copies):
        for copy in copies:
            copy.wait_recv()

    def plus(ref, *arrived):
        value = ref[...].astype(f32)
        for item in arrived:
            value = value + item.astype(f32)
        ref[...] = value.astype(bf16)

    x1, x3, x2 = turn(x, 1, NX), turn(x, -1, NX), turn(x, 2, NX)
    y1, y3, y2 = turn(y, 1, NY), turn(y, -1, NY), turn(y, 2, NY)
    few, many = pl.ds(0, 1), pl.ds(1, 2)
    front, back = pl.ds(0, 2), pl.ds(2, 2)
    n = NX * CAP * 16

    def project(*ks):
        arrive(*[pieces[k] for k in ks])
        data = [ref[at[k]].reshape(n, 2 * hw) for ref in (mine, theirs) for k in ks]
        if len(ks) > 1:
            data = [jnp.concatenate(data[:2], axis=0), jnp.concatenate(data[2:], axis=0)]
        r = None
        for i in range(4):
            a = data[i // 2][:, (i % 2) * hw : (i % 2 + 1) * hw]
            t = lax.dot_general(a, weights[i], nt, preferred_element_type=f32)
            r = t if r is None else r + t
        r = r.astype(bf16)
        for i, k in enumerate(ks):
            part = r[i * n : (i + 1) * n]
            px[at[k]] = part[:, :XCUT].reshape(NX, CAP, 16, XCUT)
            for j in range(NY):
                py[at[k], j] = part[:, XCUT + j * QUARTER : XCUT + (j + 1) * QUARTER].reshape(
                    NX, CAP, 16, QUARTER
                )
            pz[at[k]] = part[:, YCUT:].reshape(NX, CAP, 16, rest)

    class First:
        def __init__(self, axis, k):
            self.axis, self.k, self.i = axis, k, order.index(k)
            zz = at[k]
            if axis == 0:
                self.cuts = (few, many) if k % 2 else (many, few)
                self.part, self.near, self.far = px.at[zz], (x1, x3), x2
                self.r1, self.r2, self.own = rx1, rx2, x
                self.devs = (right, left)
            else:
                self.cuts = (front, back)
                self.part, self.near, self.far = py.at[zz], (y1, y3), y2
                self.r1, self.r2, self.own = ry1, ry2, y
                self.devs = (north, south)
            self.go = [
                links.send(
                    self.part.at[self.far, self.cuts[s]],
                    self.r1.at[self.i, s, pl.ds(0, self.cuts[s].size)],
                    self.devs[s],
                )
                for s in (0, 1)
            ]

        def forward(self):
            go = []
            for s in (0, 1):
                arrive(self.go[s])
                plus(
                    self.part.at[self.near[s], self.cuts[s]],
                    self.r1[self.i, s, pl.ds(0, self.cuts[s].size)],
                )
                go.append(
                    links.send(self.part.at[self.near[s]], self.r2.at[self.i, s], self.devs[s])
                )
            self.go = go

        def end(self):
            arrive(*self.go)
            plus(self.part.at[self.own], self.r2[self.i, 0], self.r2[self.i, 1])

    def block(axis, k, cut=None):
        ref = px.at[at[k], x] if axis == 0 else py.at[at[k], y]
        return ref if cut is None else ref.at[cut]

    def zcuts(axis):
        return (few, many) if axis == 0 else (pl.ds(0, 3), pl.ds(3, 1))

    def z_far(axis):
        land, land4 = (zx, zx4) if axis == 0 else (zy, zy4)
        cuts = zcuts(axis)
        go = []
        for s, d in ((0, 1), (1, -1)):
            near = links.send(block(axis, 3 * d), land.at[0, s], along[d])
            cut = cuts[1 - s]
            wide = links.send(
                block(axis, 4, cut), land4.at[s, pl.ds(0, cut.size)], along[2 * d]
            )
            go.append((near, wide))
        return go

    def z_mid(axis, go):
        land, land4 = (zx, zx4) if axis == 0 else (zy, zy4)
        cuts = zcuts(axis)
        out = []
        for s, d in ((0, 1), (1, -1)):
            near, wide = go[s]
            arrive(near)
            plus(block(axis, 2 * d), land[0, s])
            cut = cuts[1 - s]
            arrive(wide)
            plus(block(axis, 2 * d, cut), land4[s, pl.ds(0, cut.size)])
            out.append(links.send(block(axis, 2 * d), land.at[1, s], along[2 * d]))
        return out

    def z_near(axis):
        land = zx if axis == 0 else zy
        return [
            links.send(block(axis, d), land.at[2, s], along[d]) for s, d in ((0, 1), (1, -1))
        ]

    def z_sum(axis):
        land = zx if axis == 0 else zy
        value = block(axis, 0)[...].astype(f32)
        for i in (1, 2):
            for s in (0, 1):
                value = value + land[i, s].astype(f32)
        return value

    def z_ring(step, go):
        k = 4 - step
        out = []
        for s, d in ((0, 1), (1, -1)):
            cut = (front, back)[s] if step == 1 else pl.ds(0, NX)
            arrive(go[s])
            plus(pz.at[at[k * d], cut], rz[s, step - 1, cut])
            if k:
                out.append(links.send(pz.at[at[k * d]], rz.at[s, step], along[d]))
        return out

    def over_x(value, mine_ref, land):
        mine_ref[...] = value.astype(bf16)
        go = []
        for i, d in enumerate((1, 3, 2)):
            xx = turn(x, d, NX)
            go.append(links.send(mine_ref.at[xx], land.at[i], device(xx, y, z, c)))
        return go

    first = {}

    def begin(*ks):
        for k in ks:
            for axis in (0, 1):
                first[axis, k] = First(axis, k)

    def forward(*ks):
        for k in ks:
            for axis in (0, 1):
                first[axis, k].forward()

    def end(*ks):
        for axis in (0, 1):
            for k in ks:
                first[axis, k].end()

    project(4)
    begin(4)
    go_z = [
        links.send(pz.at[at[4], front], rz.at[0, 0, front], along[1]),
        links.send(pz.at[at[4], back], rz.at[1, 0, back], along[-1]),
    ]
    project(3, -3)
    begin(3, -3)
    forward(4)
    project(2, -2)
    begin(2, -2)
    go_z = z_ring(1, go_z)
    forward(3, -3)
    end(4)
    project(1, -1)
    begin(1, -1)
    go_z = z_ring(2, go_z)
    end(3, -3)
    far_x, far_y = z_far(0), z_far(1)
    forward(2, -2)
    project(0)
    begin(0)
    go_z = z_ring(3, go_z)
    end(2, -2)
    forward(1, -1)
    mid_y = z_mid(1, far_y)
    mid_x = z_mid(0, far_x)
    z_ring(4, go_z)
    end_z = over_x(pz[z].astype(f32), lz, tz)
    forward(0)
    end(1, -1)
    near_y, near_x = z_near(1), z_near(0)
    end(0)
    arrive(*mid_y, *near_y)
    end_y = over_x(z_sum(1), ly, ty)
    arrive(*mid_x, *near_x)
    total[:, :, :XCUT] = z_sum(0)
    arrive(*end_z)
    value = lz[x].astype(f32)
    for i in range(3):
        value = value + tz[i].astype(f32)
    total[:, :, XCUT + QUARTER :] = value
    arrive(*end_y)
    value = ly[x].astype(f32)
    for i in range(3):
        value = value + ty[i].astype(f32)
    total[:, :, XCUT : XCUT + QUARTER] = value

    for j in range(NY):
        for p in range(CAP):
            col[j, 4 * p : 4 * p + 4, :] = total[p, 4 * j : 4 * j + 4, :]
        col[j, 12:16, :] = jnp.zeros((4, total.shape[-1]), f32)
        col_out[j] = col[j].astype(bf16)
    ends = []
    for i, d in enumerate((1, 3, 2)):
        yy = turn(y, d, NY)
        ends.append(links.send(col_out.at[yy], col_in.at[i], device(x, yy, z, c)))
    result = col[y]

    def quarter(j):
        return pl.ds(pl.multiple_of(XCUT + j * QUARTER, 128), QUARTER)

    for p in range(CAP):
        out_ref[p, :, quarter(y)] = result[4 * p : 4 * p + 4, XCUT : XCUT + QUARTER]
    for i, d in enumerate((1, 3, 2)):
        arrive(ends[i])
        got = col_in[i].astype(f32)
        for p in range(CAP):
            out_ref[p, :, quarter(turn(y, -d, NY))] = got[4 * p : 4 * p + 4, XCUT : XCUT + QUARTER]
        result = result + got
    for p in range(CAP):
        out_ref[p, :, :XCUT] = result[4 * p : 4 * p + 4, :XCUT]
        out_ref[p, :, YCUT:] = result[4 * p : 4 * p + 4, XCUT + QUARTER :]
    links.finish()


def scatter_latents(gkv, kw, vw, kws, vws):
    width, hw = kw.shape
    rest = width - YCUT
    last = XCUT + QUARTER + rest
    hbm = pl.BlockSpec(memory_space=pltpu.HBM)

    def buffer(*shape):
        return pltpu.VMEM(shape, bf16)

    return pl.pallas_call(
        scatter_kernel,
        name="scatter_latents",
        out_shape=jax.ShapeDtypeStruct((CAP, 4, width), f32),
        in_specs=[hbm, hbm, hbm, hbm, hbm],
        out_specs=pl.BlockSpec(memory_space=pltpu.VMEM),
        scratch_shapes=[
            buffer(4, width, hw),
            buffer(NZ, NX, CAP, 16, 2 * hw),
            buffer(NZ, NX, CAP, 16, 2 * hw),
            buffer(NZ, NX, CAP, 16, XCUT),
            buffer(NZ, NY, NX, CAP, 16, QUARTER),
            buffer(NZ, NX, CAP, 16, rest),
            buffer(NZ, 2, 2, 16, XCUT),
            buffer(NZ, 2, CAP, 16, XCUT),
            buffer(NZ, 2, 2, CAP, 16, QUARTER),
            buffer(NZ, 2, NX, CAP, 16, QUARTER),
            buffer(3, 2, CAP, 16, XCUT),
            buffer(2, 2, 16, XCUT),
            buffer(3, 2, NX, CAP, 16, QUARTER),
            buffer(2, 3, CAP, 16, QUARTER),
            buffer(2, 4, NX, CAP, 16, rest),
            buffer(3, CAP, 16, QUARTER),
            buffer(3, CAP, 16, rest),
            buffer(NX, CAP, 16, QUARTER),
            buffer(NX, CAP, 16, rest),
            pltpu.VMEM((CAP, 16, last), f32),
            pltpu.VMEM((NY, 16, last), f32),
            buffer(NY, 16, last),
            buffer(3, 16, last),
            pltpu.SemaphoreType.DMA((SCATTER_SEMS,)),
            pltpu.SemaphoreType.DMA((SCATTER_SEMS,)),
            pltpu.SemaphoreType.DMA((5,)),
        ],
        compiler_params=pltpu.CompilerParams(
            collective_id=1, has_side_effects=True, vmem_limit_bytes=62 << 20
        ),
    )(gkv, kw, vw, kws, vws)


def on_device(
    latents, key_weight, value_weight, gate_logit, queries, cotangent, image_counts, token_image
):
    kw, vw = key_weight[0], value_weight[0]
    kv, kws, vws = gather_latents(latents, kw, vw)
    attended, grad_queries, gkv = attention(
        image_counts, gate_logit, token_image, kv, queries[0], cotangent[0]
    )
    grad_latents = scatter_latents(gkv, kw, vw, kws, vws)
    return attended[None], grad_queries[None], grad_latents


def solution(mesh):
    shards = P("section", None, "enc")
    return jax.shard_map(
        on_device,
        mesh=mesh,
        in_specs=(
            P("enc", "section", None), shards, shards, P("section"), shards, shards, P(), P(),
        ),
        out_specs=(shards, shards, P("enc", "section", None)),
        check_vma=False,
    )
```

```python
import math

import jax
import jax.numpy as jnp
from jax import lax
from jax.experimental import pallas as pl
from jax.experimental.pallas import tpu as pltpu
from jax.sharding import PartitionSpec as P

HD = 128
CAP = 3
NX, NY, NZ = 4, 4, 8
MESH = pl.DeviceIdType.MESH
f32 = jnp.float32
bf16 = jnp.bfloat16


def place():
    section = lax.axis_index("section")
    enc = lax.axis_index("enc")
    x = lax.rem(enc, NX)
    y = lax.rem(section // 2, NY)
    z = (enc // NX) * 2 + section // (2 * NY)
    return x, y, z, lax.rem(section, 2)


def device(x, y, z, c):
    return (lax.rem(z, 2) * (2 * NY) + y * 2 + c, (z // 2) * NX + x)


def turn(a, d, n):
    return lax.rem(a + d + n, n)


class Links:
    def __init__(self, send_sem, recv_sem):
        self.send_sem, self.recv_sem = send_sem, recv_sem
        self.used = 0
        self.sent = []

    def send(self, src, dst, dev):
        i = self.used
        self.used += 1
        copy = pltpu.make_async_remote_copy(
            src_ref=src,
            dst_ref=dst,
            send_sem=self.send_sem.at[i],
            recv_sem=self.recv_sem.at[i],
            device_id=dev,
            device_id_type=MESH,
        )
        copy.start()
        self.sent.append(copy)
        return copy

    def finish(self):
        for copy in self.sent:
            copy.wait_send()


def greet(x, y, z, c):
    peers = [device(x, turn(y, d, NY), z, c) for d in (1, 2, 3)]
    peers += [device(turn(x, d, NX), y, z, c) for d in (1, 2, 3)]
    peers += [device(x, y, turn(z, d, NZ), c) for d in (1, -1)]
    peers += [device(x, y, z, 1 - c)]
    barrier = pltpu.get_barrier_semaphore()
    for peer in peers:
        pl.semaphore_signal(barrier, inc=1, device_id=peer, device_id_type=MESH)


def meet():
    pl.semaphore_wait(pltpu.get_barrier_semaphore(), NX + NY + 1)


GATHER_SEMS = 160
XCUT, YCUT, QUARTER = 640, 1152, 128


def gather_kernel(
    own_hbm, kw_ref, vw_ref, kv_ref, theirs_ref,
    hx, hy, hz, own, mine, column, rows, weights, kv, kv_out, send_sem, recv_sem, local_sem,
):
    x, y, z, c = place()
    links = Links(send_sem, recv_sem)
    right, left = device(turn(x, 1, NX), y, z, c), device(turn(x, -1, NX), y, z, c)
    north, south = device(x, turn(y, 1, NY), z, c), device(x, turn(y, -1, NY), z, c)
    along = {d: device(x, y, turn(z, d, NZ), c) for d in (-1, 1)}
    other = device(x, y, z, 1 - c)
    width = own_hbm.shape[-1]
    hw = kw_ref.shape[-1]
    greet(x, y, z, c)
    first = pltpu.make_async_copy(own_hbm, own, local_sem.at[2])
    first.start()
    loads = [
        pltpu.make_async_copy(kw_ref, weights.at[0], local_sem.at[0]),
        pltpu.make_async_copy(vw_ref, weights.at[1], local_sem.at[1]),
    ]
    for copy in loads:
        copy.start()
    first.wait()
    for p in range(CAP):
        mine[4 * p : 4 * p + 4, :] = own[p].astype(f32)
    mine[12:16, :] = jnp.zeros((4, width), f32)
    column[y] = mine[...].astype(bf16)
    meet()

    firsts = []
    for d in (1, 3, 2):
        firsts.append(links.send(column.at[y], column.at[y], device(x, turn(y, d, NY), z, c)))

    for copy in firsts:
        copy.wait_recv()
    for j in range(NY):
        block = column[j].astype(f32)
        for p in range(CAP):
            rows[p, 4 * j : 4 * j + 4, :] = block[4 * p : 4 * p + 4, :]
    part = pl.ds(pl.multiple_of(XCUT + y * QUARTER, 128), QUARTER)
    hx[z, x] = rows[:, :, :XCUT].astype(bf16)
    hy[z, y, x] = rows[:, :, part].astype(bf16)
    hz[z, x] = rows[:, :, YCUT:].astype(bf16)

    def send(ref, dev):
        return links.send(ref, ref, dev)

    def arrive(*copies):
        for copy in copies:
            copy.wait_recv()

    stores = []
    swaps = {}

    def store(i, zz):
        j = 3 + len(stores)
        copy = pltpu.make_async_copy(kv.at[i, zz], kv_ref.at[i, zz], local_sem.at[j])
        copy.start()
        stores.append(copy)

    def project(zz):
        n = NX * CAP * 16
        data = [hx[zz].reshape(n, XCUT)]
        data += [hy[zz, j].reshape(n, QUARTER) for j in range(NY)]
        data += [hz[zz].reshape(n, width - YCUT)]
        data = jnp.concatenate(data, axis=1)
        for i in (2, 3, 0, 1):
            r = jnp.dot(data, weights[i], preferred_element_type=f32).astype(bf16)
            r = r.reshape(NX, CAP, 16, hw)
            cols = slice((i % 2) * hw, (i % 2 + 1) * hw)
            if i < 2:
                kv[c, zz, :, :, :, cols] = r
            else:
                kv_out[zz, :, :, :, cols] = r
            if i == 3:
                swaps[len(swaps)] = zz, links.send(kv_out.at[zz], kv.at[c, zz], other)
        store(c, zz)

    def swapped(i):
        zz, copy = swaps[i]
        copy.wait_recv()
        store(1 - c, zz)

    x1, x3 = turn(x, 1, NX), turn(x, -1, NX)
    y1, y3 = turn(y, 1, NY), turn(y, -1, NY)
    xpeers = [device(turn(x, d, NX), y, z, c) for d in (1, 3, 2)]
    few, many = pl.ds(0, 1), pl.ds(1, 2)
    front, back = pl.ds(0, 2), pl.ds(2, 2)

    class Last:
        def __init__(self, axis, k):
            self.axis, self.k, self.zz = axis, k, turn(z, k, NZ)
            if axis == 0:
                self.go = [send(hx.at[self.zz, x], dev) for dev in (right, left)]
            else:
                self.go = [send(hy.at[self.zz, y], dev) for dev in (north, south)]

        def forward(self):
            a, b = self.go
            if self.axis == 0:
                sa, sb = (few, many) if self.k % 2 else (many, few)
                arrive(a)
                a = send(hx.at[self.zz, x3, sa], right)
                arrive(b)
                b = send(hx.at[self.zz, x1, sb], left)
            else:
                arrive(a)
                a = send(hy.at[self.zz, y3, front], north)
                arrive(b)
                b = send(hy.at[self.zz, y1, back], south)
            self.go = [a, b]

        def end(self):
            arrive(*self.go)

    def block(axis, k, cut=None):
        zz = turn(z, k, NZ)
        ref = (hx.at[zz, x], hy.at[zz, y], hz.at[zz])[axis]
        return ref if cut is None else ref.at[cut]

    def over_z(axis):
        return [send(block(axis, 0), along[1]), send(block(axis, 0), along[-1])]

    def pass_on(axis, s, go):
        cuts = ((few, many), (pl.ds(0, 3), pl.ds(3, 1)), (front, back))[axis]
        out = []
        for i, d in ((0, -s), (1, s)):
            arrive(go[i])
            if s < 4:
                out.append(send(block(axis, d, cuts[i] if s == 3 else None), along[1 - 2 * i]))
        if axis < 2:
            for d in (-s, s) if s < 4 else (4,):
                last[axis, d] = Last(axis, d)
        return out

    for copy in loads:
        copy.wait()
    y_first = [send(hy.at[z, y, x], dev) for dev in xpeers]
    z_first = [send(hz.at[z, x], dev) for dev in xpeers]
    go_x = over_z(0)
    swap_w = [links.send(weights.at[i], weights.at[2 + i], other) for i in (0, 1)]
    last = {(0, 0): Last(0, 0)}
    arrive(*y_first)
    go_y = over_z(1)
    last[1, 0] = Last(1, 0)
    arrive(*z_first)
    go_z = over_z(2)

    def finish(k):
        project(turn(z, k, NZ))

    arrive(*swap_w)
    theirs = pltpu.make_async_copy(weights.at[pl.ds(2, 2)], theirs_ref, local_sem.at[2])
    theirs.start()

    def forward(*ks):
        for axis in (0, 1):
            for k in ks:
                last[axis, k].forward()

    def end(*ks):
        for axis in (0, 1):
            for k in ks:
                last[axis, k].end()

    go_x = pass_on(0, 1, go_x)
    go_y = pass_on(1, 1, go_y)
    go_z = pass_on(2, 1, go_z)
    forward(0)
    go_x = pass_on(0, 2, go_x)
    go_y = pass_on(1, 2, go_y)
    go_z = pass_on(2, 2, go_z)
    forward(1, -1)
    end(0)
    go_x = pass_on(0, 3, go_x)
    go_y = pass_on(1, 3, go_y)
    go_z = pass_on(2, 3, go_z)
    forward(2, -2)
    finish(0)
    end(1, -1)
    pass_on(0, 4, go_x)
    pass_on(1, 4, go_y)
    pass_on(2, 4, go_z)
    finish(1)
    forward(3, -3)
    finish(-1)
    end(2, -2)
    forward(4)
    finish(2)
    finish(-2)
    end(3, -3)
    finish(3)
    finish(-3)
    end(4)
    finish(4)

    for i in range(NZ):
        swapped(i)
    theirs.wait()
    for copy in stores:
        copy.wait()
    links.finish()


def gather_latents(latents, key_weight, value_weight):
    width = latents.shape[2]
    hw = key_weight.shape[1]
    hbm = pl.BlockSpec(memory_space=pltpu.HBM)
    return pl.pallas_call(
        gather_kernel,
        name="gather_latents",
        out_shape=(
            jax.ShapeDtypeStruct((2, NZ, NX, CAP, 16, 2 * hw), bf16),
            jax.ShapeDtypeStruct((2,) + key_weight.shape, bf16),
        ),
        in_specs=[hbm, hbm, hbm],
        out_specs=(hbm, hbm),
        scratch_shapes=[
            pltpu.VMEM((NZ, NX, CAP, 16, XCUT), bf16),
            pltpu.VMEM((NZ, NY, NX, CAP, 16, QUARTER), bf16),
            pltpu.VMEM((NZ, NX, CAP, 16, width - YCUT), bf16),
            pltpu.VMEM(latents.shape, bf16),
            pltpu.VMEM((16, width), f32),
            pltpu.VMEM((NY, 16, width), bf16),
            pltpu.VMEM((CAP, 16, width), f32),
            pltpu.VMEM((4,) + key_weight.shape, bf16),
            pltpu.VMEM((2, NZ, NX, CAP, 16, 2 * hw), bf16),
            pltpu.VMEM((NZ, NX, CAP, 16, 2 * hw), bf16),
            pltpu.SemaphoreType.DMA((GATHER_SEMS,)),
            pltpu.SemaphoreType.DMA((GATHER_SEMS,)),
            pltpu.SemaphoreType.DMA((3 + 2 * NZ,)),
        ],
        compiler_params=pltpu.CompilerParams(
            collective_id=0, has_side_effects=True, vmem_limit_bytes=62 << 20
        ),
    )(latents, key_weight, value_weight)


BLOCK = 128
CHUNK = 4
SIDE = 4


def attention_kernel(
    counts_ref, gate_ref, token_ref, kv_ref, q_hbm, cot_hbm,
    att_hbm, gq_hbm, gkv_ref,
    kvs, stage, zeros, q_ref, cot_ref, att_ref, gq_ref, gacc,
    slots, starts, chunk_of, block_of, begin_of, sem, io_sem,
):
    owners = counts_ref.shape[0]
    images = 2 * owners
    chunks = images // CHUNK
    heads = q_ref.shape[1] // HD
    hw = heads * HD
    scale = 1.0 / math.sqrt(HD)
    cols = CHUNK * 64
    tokens = q_ref.shape[0]
    pairs = chunk_of.shape[0]
    nt = (((1,), (1,)), ((), ()))

    copies = [
        pltpu.make_async_copy(q_hbm, q_ref, io_sem.at[0]),
        pltpu.make_async_copy(cot_hbm, cot_ref, io_sem.at[1]),
        pltpu.make_async_copy(att_ref, att_hbm, io_sem.at[4]),
        pltpu.make_async_copy(gq_ref, gq_hbm, io_sem.at[5]),
    ]
    zeros[...] = jnp.zeros_like(zeros)
    n = 0
    for e in range(owners):
        count = counts_ref[e]
        x, zs = e % NX, pl.ds(2 * (e // NX), 2)
        for p in range(CAP):

            @pl.when(p < count)
            def _():
                slots[n + p] = e * CAP + p
                pltpu.make_async_copy(kv_ref.at[:, zs, x, p], kvs.at[n + p], sem.at[0]).start()

            @pl.when(p >= count)
            def _():
                pltpu.make_async_copy(zeros, gkv_ref.at[:, zs, x, p], io_sem.at[2]).start()

        n = n + count
        if e == 1:
            copies[0].start()
            copies[1].start()
    token_image = token_ref[...]
    for i in range(images + 1):
        starts[i] = jnp.sum((token_image < i).astype(jnp.int32))
    factor = jnp.tanh(jnp.full((1, HD), gate_ref[0], f32))
    for i in range(pairs):
        chunk_of[i] = 0
        block_of[i] = 0
        begin_of[i] = tokens
    n = 0
    for q in range(chunks):
        b0 = starts[q * CHUNK] // BLOCK
        b1 = (starts[(q + 1) * CHUNK] + BLOCK - 1) // BLOCK

        @pl.loop(b0, b1)
        def _(b):
            i = n + b - b0
            chunk_of[i] = q
            block_of[i] = b
            begin_of[i] = b * BLOCK

        n = n + b1 - b0
    gacc[...] = jnp.zeros_like(gacc)
    copies[0].wait()
    copies[1].wait()
    pltpu.make_async_copy(kvs, kvs, sem.at[0]).wait()

    @pl.loop(0, (n + SIDE - 1) // SIDE)
    def _(step):
        work = []
        for u in range(SIDE):
            i = step * SIDE + u
            q, b, begin = chunk_of[i], block_of[i], begin_of[i]
            four = pl.ds(q * CHUNK, CHUNK)
            trows = pl.ds(pl.multiple_of(b * BLOCK, BLOCK), BLOCK)
            krows = pl.ds(pl.multiple_of(q * cols, cols), cols)
            edges = [starts[q * CHUNK + j] for j in range(CHUNK + 1)]
            which = lax.broadcasted_iota(jnp.int32, (1, cols), 1) // 64
            first = jnp.full((1, cols), edges[0], jnp.int32)
            last = jnp.full((1, cols), edges[1], jnp.int32)
            for j in range(1, CHUNK):
                first = jnp.where(which == j, edges[j], first)
                last = jnp.where(which == j, edges[j + 1], last)
            token = lax.broadcasted_iota(jnp.int32, (BLOCK, 1), 0) + begin
            here = jnp.logical_and(token >= edges[0], token < edges[CHUNK])
            wide = jnp.logical_and(token >= first, token < last).astype(f32).astype(bf16)
            lane = lax.broadcasted_iota(jnp.int32, (1, BLOCK), 1) + begin
            tall = [
                jnp.logical_and(lane >= edges[j], lane < edges[j + 1]) for j in range(CHUNK)
            ]
            ones = [t.astype(f32).astype(bf16) for t in tall]
            for h in range(heads):
                hc = slice(h * HD, (h + 1) * HD)
                vc = slice(hw + h * HD, hw + (h + 1) * HD)
                qb = q_ref[trows, hc]
                k = kvs[four, :, :, :, hc].reshape(cols, HD)
                v = kvs[four, :, :, :, vc].reshape(cols, HD)
                gm = (factor * cot_ref[trows, hc].astype(f32)).astype(bf16)
                s = lax.dot_general(k, qb, nt, preferred_element_type=f32)
                gp = lax.dot_general(v, gm, nt, preferred_element_type=f32)
                work.append((hc, vc, trows, krows, here, wide, tall, ones, qb, k, v, gm, s, gp))

        def pick(full, tall):
            out = full[(CHUNK - 1) * 64 :]
            for j in range(CHUNK - 1):
                out = jnp.where(tall[j], full[j * 64 : (j + 1) * 64], out)
            return out

        def spread(small, ones, wide):
            rows = small.astype(bf16)
            down = jnp.concatenate([rows * ones[j] for j in range(CHUNK)], axis=0)
            twice = jnp.concatenate([small, small], axis=0).T.astype(bf16)
            return down, jnp.concatenate([twice] * (CHUNK // 2), axis=1) * wide

        done = []
        for hc, vc, trows, krows, here, wide, tall, ones, qb, k, v, gm, s, gp in work:
            s = pick(s, tall)
            gp = pick(gp, tall)
            e = jnp.exp((s - jnp.max(s, axis=0, keepdims=True)) * scale)
            p = e * (1.0 / jnp.sum(e, axis=0, keepdims=True))
            w = jnp.sum(p * gp, axis=0, keepdims=True)
            gs = p * (gp - w) * scale
            p_down, p_wide = spread(p, ones, wide)
            gs_down, gs_wide = spread(gs, ones, wide)
            done.append((
                jnp.dot(p_wide, v, preferred_element_type=f32),
                jnp.dot(gs_wide, k, preferred_element_type=f32),
                jnp.dot(gs_down, qb, preferred_element_type=f32),
                jnp.dot(p_down, gm, preferred_element_type=f32),
            ))
        for item, (mix, gq, gk, gv) in zip(work, done):
            hc, vc, trows, krows, here = item[:5]
            att_ref[trows, hc] = jnp.where(here, (factor * mix).astype(bf16), att_ref[trows, hc])
            gq_ref[trows, hc] = jnp.where(here, gq.astype(bf16), gq_ref[trows, hc])
            gacc[krows, hc] += gk
            gacc[krows, vc] += gv

    copies[2].start()
    copies[3].start()

    @pl.loop(0, chunks)
    def _(q):
        krows = pl.ds(pl.multiple_of(q * cols, cols), cols)
        stage[pl.ds(q * CHUNK, CHUNK)] = (
            gacc[krows, :].astype(bf16).reshape(CHUNK, 2, 2, 16, 2 * hw)
        )
        for j in range(CHUNK):
            i = q * CHUNK + j
            slot = slots[i]
            enc = slot // CAP
            pltpu.make_async_copy(
                stage.at[i],
                gkv_ref.at[:, pl.ds(2 * (enc // NX), 2), lax.rem(enc, NX), slot - enc * CAP],
                io_sem.at[3],
            ).start()

    empty = stage.at[pl.ds(0, CAP * owners - images)]
    pltpu.make_async_copy(empty, empty, io_sem.at[2]).wait()
    pltpu.make_async_copy(stage, stage, io_sem.at[3]).wait()
    copies[2].wait()
    copies[3].wait()


def attention(image_counts, gate_logit, token_image, kv, queries, cotangent):
    tokens, hw = queries.shape
    images = 2 * image_counts.shape[0]
    pairs = images // CHUNK + tokens // BLOCK
    vmem = pl.BlockSpec(memory_space=pltpu.VMEM)
    smem = pl.BlockSpec(memory_space=pltpu.SMEM)
    hbm = pl.BlockSpec(memory_space=pltpu.HBM)
    return pl.pallas_call(
        attention_kernel,
        name="attention",
        out_shape=(
            jax.ShapeDtypeStruct((tokens, hw), bf16),
            jax.ShapeDtypeStruct((tokens, hw), bf16),
            jax.ShapeDtypeStruct((2, NZ, NX, CAP, 16, 2 * hw), bf16),
        ),
        in_specs=[smem, smem, vmem, hbm, hbm, hbm],
        out_specs=(hbm, hbm, hbm),
        scratch_shapes=[
            pltpu.VMEM((images, 2, 2, 16, 2 * hw), bf16),
            pltpu.VMEM((images, 2, 2, 16, 2 * hw), bf16),
            pltpu.VMEM((2, 2, 16, 2 * hw), bf16),
            pltpu.VMEM((tokens, hw), bf16),
            pltpu.VMEM((tokens, hw), bf16),
            pltpu.VMEM((tokens, hw), bf16),
            pltpu.VMEM((tokens, hw), bf16),
            pltpu.VMEM((images * 64, 2 * hw), f32),
            pltpu.SMEM((images,), jnp.int32),
            pltpu.SMEM((images + 1,), jnp.int32),
            pltpu.SMEM((pairs,), jnp.int32),
            pltpu.SMEM((pairs,), jnp.int32),
            pltpu.SMEM((pairs,), jnp.int32),
            pltpu.SemaphoreType.DMA((1,)),
            pltpu.SemaphoreType.DMA((6,)),
        ],
        compiler_params=pltpu.CompilerParams(vmem_limit_bytes=62 << 20),
    )(image_counts, gate_logit, token_image.reshape(8, tokens // 8), kv, queries, cotangent)


SCATTER_SEMS = 128


def scatter_kernel(
    gkv_ref, kw_hbm, vw_hbm, theirs_hbm, out_ref,
    weights, mine, theirs, px, py, pz, rx1, rx2, ry1, ry2, zx, zx4, zy, zy4, rz, rz4, ty, ly, tz, lz,
    total, col, col_x, col_yz, in_x, in_yz, send_sem, recv_sem, local_sem,
):
    x, y, z, c = place()
    links = Links(send_sem, recv_sem)
    right, left = device(turn(x, 1, NX), y, z, c), device(turn(x, -1, NX), y, z, c)
    north, south = device(x, turn(y, 1, NY), z, c), device(x, turn(y, -1, NY), z, c)
    along = {d: device(x, y, turn(z, d, NZ), c) for d in (-1, 1)}
    other = device(x, y, z, 1 - c)
    hw = kw_hbm.shape[1]
    width = kw_hbm.shape[0]
    nt = (((1,), (1,)), ((), ()))
    greet(x, y, z, c)
    loads = [pltpu.make_async_copy(gkv_ref.at[c], mine, local_sem.at[0])]
    for i, ref in enumerate((kw_hbm, vw_hbm, theirs_hbm.at[0], theirs_hbm.at[1])):
        loads.append(pltpu.make_async_copy(ref, weights.at[i], local_sem.at[1 + i]))
    for copy in loads:
        copy.start()
    meet()
    order = (4, 3, -3, 2, -2, 1, -1, 0)
    at = {k: turn(z, k, NZ) for k in order}
    pieces = {k: links.send(gkv_ref.at[1 - c, at[k]], theirs.at[at[k]], other) for k in order}
    for copy in loads:
        copy.wait()

    def arrive(*copies):
        for copy in copies:
            copy.wait_recv()

    def plus(ref, *arrived):
        value = ref[...].astype(f32)
        for item in arrived:
            value = value + item.astype(f32)
        ref[...] = value.astype(bf16)

    x1, x3, x2 = turn(x, 1, NX), turn(x, -1, NX), turn(x, 2, NX)
    y1, y3, y2 = turn(y, 1, NY), turn(y, -1, NY), turn(y, 2, NY)
    few, many = pl.ds(0, 1), pl.ds(1, 2)
    front, back = pl.ds(0, 2), pl.ds(2, 2)
    n = NX * CAP * 16

    def project(*ks):
        arrive(*[pieces[k] for k in ks])
        data = [ref[at[k]].reshape(n, 2 * hw) for ref in (mine, theirs) for k in ks]
        if len(ks) > 1:
            data = [jnp.concatenate(data[:2], axis=0), jnp.concatenate(data[2:], axis=0)]
        r = None
        for i in range(4):
            a = data[i // 2][:, (i % 2) * hw : (i % 2 + 1) * hw]
            t = lax.dot_general(a, weights[i], nt, preferred_element_type=f32)
            r = t if r is None else r + t
        r = r.astype(bf16)
        for i, k in enumerate(ks):
            part = r[i * n : (i + 1) * n]
            px[at[k]] = part[:, :XCUT].reshape(NX, CAP, 16, XCUT)
            pz[at[k]] = part[:, YCUT:].reshape(NX, CAP, 16, width - YCUT)
            for j in range(NY):
                py[at[k], j] = part[:, XCUT + j * QUARTER : XCUT + (j + 1) * QUARTER].reshape(
                    NX, CAP, 16, QUARTER
                )

    class First:
        def __init__(self, axis, k):
            self.axis, self.k, self.i = axis, k, order.index(k)
            zz = at[k]
            if axis == 0:
                self.cuts = (few, many) if k % 2 else (many, few)
                self.part, self.near, self.far = px.at[zz], (x1, x3), x2
                self.r1, self.r2, self.own = rx1, rx2, x
                self.devs = (right, left)
            else:
                self.cuts = (front, back)
                self.part, self.near, self.far = py.at[zz], (y1, y3), y2
                self.r1, self.r2, self.own = ry1, ry2, y
                self.devs = (north, south)
            self.go = [
                links.send(
                    self.part.at[self.far, self.cuts[s]],
                    self.r1.at[self.i, s, pl.ds(0, self.cuts[s].size)],
                    self.devs[s],
                )
                for s in (0, 1)
            ]

        def forward(self):
            go = []
            for s in (0, 1):
                arrive(self.go[s])
                plus(
                    self.part.at[self.near[s], self.cuts[s]],
                    self.r1[self.i, s, pl.ds(0, self.cuts[s].size)],
                )
                go.append(
                    links.send(self.part.at[self.near[s]], self.r2.at[self.i, s], self.devs[s])
                )
            self.go = go

        def end(self):
            arrive(*self.go)
            plus(self.part.at[self.own], self.r2[self.i, 0], self.r2[self.i, 1])

    def block(axis, k, cut=None):
        ref = (px.at[at[k], x], py.at[at[k], y], pz.at[at[k]])[axis]
        return ref if cut is None else ref.at[cut]

    def zcuts(axis):
        return ((few, many), (pl.ds(0, 3), pl.ds(3, 1)), (front, back))[axis]

    def z_send(axis, k, go):
        land, land4 = ((zx, zx4), (zy, zy4), (rz, rz4))[axis]
        out = []
        for s, d in ((0, 1), (1, -1)):
            cut = zcuts(axis)[s]
            if k == 4:
                out.append(links.send(block(axis, 4, cut), land4.at[s, pl.ds(0, cut.size)], along[d]))
                continue
            arrive(go[s])
            if k == 3:
                plus(block(axis, 3 * d, cut), land4[s, pl.ds(0, cut.size)])
            else:
                plus(block(axis, k * d), land[2 - k, s])
            out.append(links.send(block(axis, k * d), land.at[3 - k, s], along[d]))
        return out

    def z_sum(axis, go):
        land = (zx, zy, rz)[axis]
        arrive(*go)
        value = block(axis, 0)[...].astype(f32)
        for s in (0, 1):
            value = value + land[2, s].astype(f32)
        return value

    def over_x(value, mine_ref, land):
        mine_ref[...] = value.astype(bf16)
        go = []
        for i, d in enumerate((1, 3, 2)):
            xx = turn(x, d, NX)
            go.append(links.send(mine_ref.at[xx], land.at[i], device(xx, y, z, c)))
        return go

    first = {}

    def begin(*ks):
        for k in ks:
            for axis in (1, 0):
                first[axis, k] = First(axis, k)

    def forward(*ks):
        for k in ks:
            for axis in (1, 0):
                first[axis, k].forward()

    def end(*ks):
        for axis in (1, 0):
            for k in ks:
                first[axis, k].end()

    project(4)
    begin(4)
    go_z = z_send(2, 4, None)
    project(3, -3)
    begin(3, -3)
    forward(4)
    go_z = z_send(2, 3, go_z)
    project(2, -2)
    begin(2, -2)
    forward(3, -3)
    end(4)
    go_y, go_x = z_send(1, 4, None), z_send(0, 4, None)
    go_z = z_send(2, 2, go_z)
    project(1, -1)
    begin(1, -1)
    end(3, -3)
    go_y, go_x = z_send(1, 3, go_y), z_send(0, 3, go_x)
    go_z = z_send(2, 1, go_z)
    forward(2, -2)
    project(0)
    begin(0)
    end(2, -2)
    go_y, go_x = z_send(1, 2, go_y), z_send(0, 2, go_x)
    end_z = over_x(z_sum(2, go_z), lz, tz)
    forward(1, -1)
    forward(0)
    end(1, -1)
    go_y, go_x = z_send(1, 1, go_y), z_send(0, 1, go_x)
    end(0)
    end_y = over_x(z_sum(1, go_y), ly, ty)

    def over_y(cols, cut):
        for j in range(NY):
            for p in range(CAP):
                col[j, 4 * p : 4 * p + 4, cols] = total[p, 4 * j : 4 * j + 4, cols]
            col[j, 12:16, cols] = jnp.zeros((4, cols.stop - cols.start), f32)
            (col_x, col_yz)[cut][j] = col[j, :, cols].astype(bf16)
        out, land = ((col_x, in_x), (col_yz, in_yz))[cut]
        ends = []
        for i, d in enumerate((1, 3, 2)):
            yy = turn(y, d, NY)
            ends.append(links.send(out.at[yy], land.at[i], device(x, yy, z, c)))
        return ends

    xs, yzs = slice(0, XCUT), slice(XCUT, total.shape[-1])
    total[:, :, xs] = z_sum(0, go_x)
    end_x = over_y(xs, 0)
    for cols, ends, own, land in (
        (slice(XCUT + QUARTER, total.shape[-1]), end_z, lz, tz),
        (slice(XCUT, XCUT + QUARTER), end_y, ly, ty),
    ):
        arrive(*ends)
        value = own[x].astype(f32)
        for i in range(3):
            value = value + land[i].astype(f32)
        total[:, :, cols] = value
    end_yz = over_y(yzs, 1)

    def quarter(j):
        return pl.ds(pl.multiple_of(XCUT + j * QUARTER, 128), QUARTER)

    arrive(*end_x)
    result = col[y, :, xs]
    for i in range(3):
        result = result + in_x[i].astype(f32)
    for p in range(CAP):
        out_ref[p, :, :XCUT] = result[4 * p : 4 * p + 4]
    result = col[y, :, yzs]
    for p in range(CAP):
        out_ref[p, :, quarter(y)] = result[4 * p : 4 * p + 4, :QUARTER]
    for i, d in enumerate((1, 3, 2)):
        arrive(end_yz[i])
        got = in_yz[i].astype(f32)
        for p in range(CAP):
            out_ref[p, :, quarter(turn(y, -d, NY))] = got[4 * p : 4 * p + 4, :QUARTER]
        result = result + got
    for p in range(CAP):
        out_ref[p, :, YCUT:] = result[4 * p : 4 * p + 4, QUARTER:]
    links.finish()


def scatter_latents(gkv, kw, vw, theirs):
    width, hw = kw.shape
    rest = width - YCUT
    last = XCUT + QUARTER + rest
    hbm = pl.BlockSpec(memory_space=pltpu.HBM)

    def buffer(*shape):
        return pltpu.VMEM(shape, bf16)

    return pl.pallas_call(
        scatter_kernel,
        name="scatter_latents",
        out_shape=jax.ShapeDtypeStruct((CAP, 4, width), f32),
        in_specs=[hbm, hbm, hbm, hbm],
        out_specs=pl.BlockSpec(memory_space=pltpu.VMEM),
        scratch_shapes=[
            buffer(4, width, hw),
            buffer(NZ, NX, CAP, 16, 2 * hw),
            buffer(NZ, NX, CAP, 16, 2 * hw),
            buffer(NZ, NX, CAP, 16, XCUT),
            buffer(NZ, NY, NX, CAP, 16, QUARTER),
            buffer(NZ, NX, CAP, 16, rest),
            buffer(NZ, 2, 2, 16, XCUT),
            buffer(NZ, 2, CAP, 16, XCUT),
            buffer(NZ, 2, 2, CAP, 16, QUARTER),
            buffer(NZ, 2, NX, CAP, 16, QUARTER),
            buffer(3, 2, CAP, 16, XCUT),
            buffer(2, 2, 16, XCUT),
            buffer(3, 2, NX, CAP, 16, QUARTER),
            buffer(2, 3, CAP, 16, QUARTER),
            buffer(3, 2, NX, CAP, 16, rest),
            buffer(2, 2, CAP, 16, rest),
            buffer(3, CAP, 16, QUARTER),
            buffer(NX, CAP, 16, QUARTER),
            buffer(3, CAP, 16, rest),
            buffer(NX, CAP, 16, rest),
            pltpu.VMEM((CAP, 16, last), f32),
            pltpu.VMEM((NY, 16, last), f32),
            buffer(NY, 16, XCUT),
            buffer(NY, 16, QUARTER + rest),
            buffer(3, 16, XCUT),
            buffer(3, 16, QUARTER + rest),
            pltpu.SemaphoreType.DMA((SCATTER_SEMS,)),
            pltpu.SemaphoreType.DMA((SCATTER_SEMS,)),
            pltpu.SemaphoreType.DMA((5,)),
        ],
        compiler_params=pltpu.CompilerParams(
            collective_id=1, has_side_effects=True, vmem_limit_bytes=52 << 20
        ),
    )(gkv, kw, vw, theirs)


def on_device(
    latents, key_weight, value_weight, gate_logit, queries, cotangent, image_counts, token_image
):
    kw, vw = key_weight[0], value_weight[0]
    kv, theirs = gather_latents(latents, kw, vw)
    attended, grad_queries, gkv = attention(
        image_counts, gate_logit, token_image, kv, queries[0], cotangent[0]
    )
    grad_latents = scatter_latents(gkv, kw, vw, theirs)
    return attended[None], grad_queries[None], grad_latents


def solution(mesh):
    shards = P("section", None, "enc")
    return jax.shard_map(
        on_device,
        mesh=mesh,
        in_specs=(
            P("enc", "section", None), shards, shards, P("section"), shards, shards, P(), P(),
        ),
        out_specs=(shards, shards, P("enc", "section", None)),
        check_vma=False,
    )
```

```python
import math

import jax
import jax.numpy as jnp
from jax import lax
from jax.experimental import pallas as pl
from jax.experimental.pallas import tpu as pltpu
from jax.sharding import PartitionSpec as P

HD = 128
CAP = 3
NX, NY, NZ = 4, 4, 8
MESH = pl.DeviceIdType.MESH
f32 = jnp.float32
bf16 = jnp.bfloat16


def place():
    section = lax.axis_index("section")
    enc = lax.axis_index("enc")
    x = lax.rem(enc, NX)
    y = lax.rem(section // 2, NY)
    z = (enc // NX) * 2 + section // (2 * NY)
    return x, y, z, lax.rem(section, 2)


def device(x, y, z, c):
    return (lax.rem(z, 2) * (2 * NY) + y * 2 + c, (z // 2) * NX + x)


def turn(a, d, n):
    return lax.rem(a + d + n, n)


class Links:
    def __init__(self, send_sem, recv_sem):
        self.send_sem, self.recv_sem = send_sem, recv_sem
        self.used = 0
        self.sent = []

    def send(self, src, dst, dev):
        i = self.used
        self.used += 1
        copy = pltpu.make_async_remote_copy(
            src_ref=src,
            dst_ref=dst,
            send_sem=self.send_sem.at[i],
            recv_sem=self.recv_sem.at[i],
            device_id=dev,
            device_id_type=MESH,
        )
        copy.start()
        self.sent.append(copy)
        return copy

    def finish(self):
        for copy in self.sent:
            copy.wait_send()


STEPS = [(dx, dy) for dx in range(NX) for dy in range(NY) if dx or dy]


def greet(x, y, z, c):
    peers = [device(turn(x, dx, NX), turn(y, dy, NY), z, c) for dx, dy in STEPS]
    peers += [device(x, y, turn(z, d, NZ), c) for d in (1, -1)]
    peers += [device(x, y, z, 1 - c)]
    barrier = pltpu.get_barrier_semaphore()
    for peer in peers:
        pl.semaphore_signal(barrier, inc=1, device_id=peer, device_id_type=MESH)


def meet():
    pl.semaphore_wait(pltpu.get_barrier_semaphore(), len(STEPS) + 3)


GATHER_SEMS = 160
XCUT, YCUT, QUARTER = 640, 1152, 128


def gather_kernel(
    own_hbm, kw_ref, vw_ref, kv_ref, theirs_ref,
    hx, hy, hz, own, mine, column, rows, out_yz, in_yz, rows_yz, weights, kv, kv_out, send_sem, recv_sem, local_sem,
):
    x, y, z, c = place()
    links = Links(send_sem, recv_sem)
    right, left = device(turn(x, 1, NX), y, z, c), device(turn(x, -1, NX), y, z, c)
    north, south = device(x, turn(y, 1, NY), z, c), device(x, turn(y, -1, NY), z, c)
    along = {d: device(x, y, turn(z, d, NZ), c) for d in (-1, 1)}
    other = device(x, y, z, 1 - c)
    width = own_hbm.shape[-1]
    hw = kw_ref.shape[-1]
    greet(x, y, z, c)
    first = pltpu.make_async_copy(own_hbm, own, local_sem.at[2])
    first.start()
    loads = [
        pltpu.make_async_copy(kw_ref, weights.at[0], local_sem.at[0]),
        pltpu.make_async_copy(vw_ref, weights.at[1], local_sem.at[1]),
    ]
    for copy in loads:
        copy.start()
    first.wait()
    for p in range(CAP):
        mine[4 * p : 4 * p + 4, :] = own[p].astype(f32)
    mine[12:16, :] = jnp.zeros((4, width), f32)
    column[y] = mine[:, :XCUT].astype(bf16)
    for j in range(NY):
        out_yz[j, 0] = mine[:, XCUT + j * QUARTER : XCUT + (j + 1) * QUARTER].astype(bf16)
        out_yz[j, 1] = mine[:, YCUT:].astype(bf16)
    meet()

    firsts = []
    for d in (1, 3, 2):
        firsts.append(links.send(column.at[y], column.at[y], device(x, turn(y, d, NY), z, c)))
    seconds = []
    for dx, dy in STEPS:
        xx, yy = turn(x, dx, NX), turn(y, dy, NY)
        seconds.append(links.send(out_yz.at[yy], in_yz.at[x, y], device(xx, yy, z, c)))
    in_yz[x, y] = out_yz[y]
    for copy in firsts:
        copy.wait_recv()
    for j in range(NY):
        piece = column[j].astype(f32)
        for p in range(CAP):
            rows[p, 4 * j : 4 * j + 4, :] = piece[4 * p : 4 * p + 4, :]
    hx[z, x] = rows[...].astype(bf16)

    def send(ref, dev):
        return links.send(ref, ref, dev)

    def arrive(*copies):
        for copy in copies:
            copy.wait_recv()

    stores = []
    swaps = []

    def store(zz):
        j = 3 + len(stores)
        copy = pltpu.make_async_copy(kv.at[zz], kv_ref.at[c, zz], local_sem.at[j])
        copy.start()
        stores.append(copy)

    def project(zz):
        n = NX * CAP * 16
        data = [hx[zz].reshape(n, XCUT)]
        data += [hy[zz, j].reshape(n, QUARTER) for j in range(NY)]
        data += [hz[zz].reshape(n, width - YCUT)]
        data = jnp.concatenate(data, axis=1)
        for i in (2, 3, 0, 1):
            r = jnp.dot(data, weights[i], preferred_element_type=f32).astype(bf16)
            r = r.reshape(NX, CAP, 16, hw)
            cols = slice((i % 2) * hw, (i % 2 + 1) * hw)
            if i < 2:
                kv[zz, :, :, :, cols] = r
            else:
                kv_out[zz, :, :, :, cols] = r
            if i == 3:
                swaps.append(links.send(kv_out.at[zz], kv_ref.at[c, zz], other))
        store(zz)

    x1, x3 = turn(x, 1, NX), turn(x, -1, NX)
    y1, y3 = turn(y, 1, NY), turn(y, -1, NY)
    few, many = pl.ds(0, 1), pl.ds(1, 2)
    front, back = pl.ds(0, 2), pl.ds(2, 2)

    class Last:
        def __init__(self, axis, k):
            self.axis, self.k, self.zz = axis, k, turn(z, k, NZ)
            if axis == 0:
                self.go = [send(hx.at[self.zz, x], dev) for dev in (right, left)]
            else:
                self.go = [send(hy.at[self.zz, y], dev) for dev in (north, south)]

        def forward(self):
            a, b = self.go
            if self.axis == 0:
                sa, sb = (few, many) if self.k % 2 else (many, few)
                arrive(a)
                a = send(hx.at[self.zz, x3, sa], right)
                arrive(b)
                b = send(hx.at[self.zz, x1, sb], left)
            else:
                arrive(a)
                a = send(hy.at[self.zz, y3, front], north)
                arrive(b)
                b = send(hy.at[self.zz, y1, back], south)
            self.go = [a, b]

        def end(self):
            arrive(*self.go)

    def block(axis, k, cut=None):
        zz = turn(z, k, NZ)
        ref = (hx.at[zz, x], hy.at[zz, y], hz.at[zz])[axis]
        return ref if cut is None else ref.at[cut]

    def over_z(axis):
        return [send(block(axis, 0), along[1]), send(block(axis, 0), along[-1])]

    def pass_on(axis, s, go):
        cuts = ((few, many), (pl.ds(0, 3), pl.ds(3, 1)), (front, back))[axis]
        out = []
        for i, d in ((0, -s), (1, s)):
            arrive(go[i])
            if s < 4:
                out.append(send(block(axis, d, cuts[i] if s == 3 else None), along[1 - 2 * i]))
        if axis < 2:
            for d in (-s, s) if s < 4 else (4,):
                last[axis, d] = Last(axis, d)
        return out

    for copy in loads:
        copy.wait()
    go_x = over_z(0)
    swap_w = [links.send(weights.at[i], weights.at[2 + i], other) for i in (0, 1)]
    last = {(0, 0): Last(0, 0)}
    arrive(*seconds)
    for i in range(NX):
        for j in range(NY):
            piece = in_yz[i, j].astype(f32)
            for p in range(CAP):
                for s in range(2):
                    rows_yz[s, p, 4 * j : 4 * j + 4, :] = piece[s, 4 * p : 4 * p + 4, :]
        hy[z, y, i] = rows_yz[0].astype(bf16)
        hz[z, i] = rows_yz[1].astype(bf16)
    go_y = over_z(1)
    last[1, 0] = Last(1, 0)
    go_z = over_z(2)

    def finish(k):
        project(turn(z, k, NZ))

    arrive(*swap_w)
    theirs = pltpu.make_async_copy(weights.at[pl.ds(2, 2)], theirs_ref, local_sem.at[2])
    theirs.start()

    def forward(*ks):
        for axis in (0, 1):
            for k in ks:
                last[axis, k].forward()

    def end(*ks):
        for axis in (0, 1):
            for k in ks:
                last[axis, k].end()

    go_x = pass_on(0, 1, go_x)
    go_y = pass_on(1, 1, go_y)
    go_z = pass_on(2, 1, go_z)
    forward(0)
    go_x = pass_on(0, 2, go_x)
    go_y = pass_on(1, 2, go_y)
    go_z = pass_on(2, 2, go_z)
    forward(1, -1)
    end(0)
    go_x = pass_on(0, 3, go_x)
    go_y = pass_on(1, 3, go_y)
    go_z = pass_on(2, 3, go_z)
    forward(2, -2)
    finish(0)
    end(1, -1)
    pass_on(0, 4, go_x)
    pass_on(1, 4, go_y)
    pass_on(2, 4, go_z)
    finish(1)
    forward(3, -3)
    finish(-1)
    end(2, -2)
    forward(4)
    finish(2)
    finish(-2)
    end(3, -3)
    finish(3)
    finish(-3)
    end(4)
    finish(4)

    arrive(*swaps)
    theirs.wait()
    for copy in stores:
        copy.wait()
    links.finish()


def gather_latents(latents, key_weight, value_weight):
    width = latents.shape[2]
    hw = key_weight.shape[1]
    hbm = pl.BlockSpec(memory_space=pltpu.HBM)
    return pl.pallas_call(
        gather_kernel,
        name="gather_latents",
        out_shape=(
            jax.ShapeDtypeStruct((2, NZ, NX, CAP, 16, 2 * hw), bf16),
            jax.ShapeDtypeStruct((2,) + key_weight.shape, bf16),
        ),
        in_specs=[hbm, hbm, hbm],
        out_specs=(hbm, hbm),
        scratch_shapes=[
            pltpu.VMEM((NZ, NX, CAP, 16, XCUT), bf16),
            pltpu.VMEM((NZ, NY, NX, CAP, 16, QUARTER), bf16),
            pltpu.VMEM((NZ, NX, CAP, 16, width - YCUT), bf16),
            pltpu.VMEM(latents.shape, bf16),
            pltpu.VMEM((16, width), f32),
            pltpu.VMEM((NY, 16, XCUT), bf16),
            pltpu.VMEM((CAP, 16, XCUT), f32),
            pltpu.VMEM((NY, 2, 16, QUARTER), bf16),
            pltpu.VMEM((NX, NY, 2, 16, QUARTER), bf16),
            pltpu.VMEM((2, CAP, 16, QUARTER), f32),
            pltpu.VMEM((4,) + key_weight.shape, bf16),
            pltpu.VMEM((NZ, NX, CAP, 16, 2 * hw), bf16),
            pltpu.VMEM((NZ, NX, CAP, 16, 2 * hw), bf16),
            pltpu.SemaphoreType.DMA((GATHER_SEMS,)),
            pltpu.SemaphoreType.DMA((GATHER_SEMS,)),
            pltpu.SemaphoreType.DMA((3 + NZ,)),
        ],
        compiler_params=pltpu.CompilerParams(
            collective_id=0, has_side_effects=True, vmem_limit_bytes=62 << 20
        ),
    )(latents, key_weight, value_weight)


BLOCK = 128
CHUNK = 4
SIDE = 4


def attention_kernel(
    counts_ref, gate_ref, token_ref, kv_ref, q_hbm, cot_hbm,
    att_hbm, gq_hbm, gkv_ref,
    kvs, stage, zeros, q_ref, cot_ref, att_ref, gq_ref, gacc,
    slots, starts, chunk_of, block_of, begin_of, sem, io_sem,
):
    owners = counts_ref.shape[0]
    images = 2 * owners
    chunks = images // CHUNK
    heads = q_ref.shape[1] // HD
    hw = heads * HD
    scale = 1.0 / math.sqrt(HD)
    cols = CHUNK * 64
    tokens = q_ref.shape[0]
    pairs = chunk_of.shape[0]
    nt = (((1,), (1,)), ((), ()))

    copies = [
        pltpu.make_async_copy(q_hbm, q_ref, io_sem.at[0]),
        pltpu.make_async_copy(cot_hbm, cot_ref, io_sem.at[1]),
        pltpu.make_async_copy(att_ref, att_hbm, io_sem.at[4]),
        pltpu.make_async_copy(gq_ref, gq_hbm, io_sem.at[5]),
    ]
    zeros[...] = jnp.zeros_like(zeros)
    n = 0
    for e in range(owners):
        count = counts_ref[e]
        x, zs = e % NX, pl.ds(2 * (e // NX), 2)
        for p in range(CAP):

            @pl.when(p < count)
            def _():
                slots[n + p] = e * CAP + p
                pltpu.make_async_copy(kv_ref.at[:, zs, x, p], kvs.at[n + p], sem.at[0]).start()

            @pl.when(p >= count)
            def _():
                pltpu.make_async_copy(zeros, gkv_ref.at[:, zs, x, p], io_sem.at[2]).start()

        n = n + count
        if e == 1:
            copies[0].start()
            copies[1].start()
    token_image = token_ref[...]
    for i in range(images + 1):
        starts[i] = jnp.sum((token_image < i).astype(jnp.int32))
    factor = jnp.tanh(jnp.full((1, HD), gate_ref[0], f32))
    for i in range(pairs):
        chunk_of[i] = 0
        block_of[i] = 0
        begin_of[i] = tokens
    n = 0
    for q in range(chunks):
        b0 = starts[q * CHUNK] // BLOCK
        b1 = (starts[(q + 1) * CHUNK] + BLOCK - 1) // BLOCK

        @pl.loop(b0, b1)
        def _(b):
            i = n + b - b0
            chunk_of[i] = q
            block_of[i] = b
            begin_of[i] = b * BLOCK

        n = n + b1 - b0
    gacc[...] = jnp.zeros_like(gacc)
    copies[0].wait()
    copies[1].wait()
    pltpu.make_async_copy(kvs, kvs, sem.at[0]).wait()

    @pl.loop(0, (n + SIDE - 1) // SIDE)
    def _(step):
        work = []
        for u in range(SIDE):
            i = step * SIDE + u
            q, b, begin = chunk_of[i], block_of[i], begin_of[i]
            four = pl.ds(q * CHUNK, CHUNK)
            trows = pl.ds(pl.multiple_of(b * BLOCK, BLOCK), BLOCK)
            krows = pl.ds(pl.multiple_of(q * cols, cols), cols)
            edges = [starts[q * CHUNK + j] for j in range(CHUNK + 1)]
            which = lax.broadcasted_iota(jnp.int32, (1, cols), 1) // 64
            first = jnp.full((1, cols), edges[0], jnp.int32)
            last = jnp.full((1, cols), edges[1], jnp.int32)
            for j in range(1, CHUNK):
                first = jnp.where(which == j, edges[j], first)
                last = jnp.where(which == j, edges[j + 1], last)
            token = lax.broadcasted_iota(jnp.int32, (BLOCK, 1), 0) + begin
            here = jnp.logical_and(token >= edges[0], token < edges[CHUNK])
            wide = jnp.logical_and(token >= first, token < last).astype(f32).astype(bf16)
            lane = lax.broadcasted_iota(jnp.int32, (1, BLOCK), 1) + begin
            tall = [
                jnp.logical_and(lane >= edges[j], lane < edges[j + 1]) for j in range(CHUNK)
            ]
            ones = [t.astype(f32).astype(bf16) for t in tall]
            for h in range(heads):
                hc = slice(h * HD, (h + 1) * HD)
                vc = slice(hw + h * HD, hw + (h + 1) * HD)
                qb = q_ref[trows, hc]
                k = kvs[four, :, :, :, hc].reshape(cols, HD)
                v = kvs[four, :, :, :, vc].reshape(cols, HD)
                gm = (factor * cot_ref[trows, hc].astype(f32)).astype(bf16)
                s = lax.dot_general(k, qb, nt, preferred_element_type=f32)
                gp = lax.dot_general(v, gm, nt, preferred_element_type=f32)
                work.append((hc, vc, trows, krows, here, wide, tall, ones, qb, k, v, gm, s, gp))

        def pick(full, tall):
            out = full[(CHUNK - 1) * 64 :]
            for j in range(CHUNK - 1):
                out = jnp.where(tall[j], full[j * 64 : (j + 1) * 64], out)
            return out

        def spread(small, ones, wide):
            rows = small.astype(bf16)
            down = jnp.concatenate([rows * ones[j] for j in range(CHUNK)], axis=0)
            twice = jnp.concatenate([small, small], axis=0).T.astype(bf16)
            return down, jnp.concatenate([twice] * (CHUNK // 2), axis=1) * wide

        done = []
        for hc, vc, trows, krows, here, wide, tall, ones, qb, k, v, gm, s, gp in work:
            s = pick(s, tall)
            gp = pick(gp, tall)
            e = jnp.exp((s - jnp.max(s, axis=0, keepdims=True)) * scale)
            p = e * (1.0 / jnp.sum(e, axis=0, keepdims=True))
            w = jnp.sum(p * gp, axis=0, keepdims=True)
            gs = p * (gp - w) * scale
            p_down, p_wide = spread(p, ones, wide)
            gs_down, gs_wide = spread(gs, ones, wide)
            done.append((
                jnp.dot(p_wide, v, preferred_element_type=f32),
                jnp.dot(gs_wide, k, preferred_element_type=f32),
                jnp.dot(gs_down, qb, preferred_element_type=f32),
                jnp.dot(p_down, gm, preferred_element_type=f32),
            ))
        for item, (mix, gq, gk, gv) in zip(work, done):
            hc, vc, trows, krows, here = item[:5]
            att_ref[trows, hc] = jnp.where(here, (factor * mix).astype(bf16), att_ref[trows, hc])
            gq_ref[trows, hc] = jnp.where(here, gq.astype(bf16), gq_ref[trows, hc])
            gacc[krows, hc] += gk
            gacc[krows, vc] += gv

    copies[2].start()
    copies[3].start()

    @pl.loop(0, chunks)
    def _(q):
        krows = pl.ds(pl.multiple_of(q * cols, cols), cols)
        stage[pl.ds(q * CHUNK, CHUNK)] = (
            gacc[krows, :].astype(bf16).reshape(CHUNK, 2, 2, 16, 2 * hw)
        )
        for j in range(CHUNK):
            i = q * CHUNK + j
            slot = slots[i]
            enc = slot // CAP
            pltpu.make_async_copy(
                stage.at[i],
                gkv_ref.at[:, pl.ds(2 * (enc // NX), 2), lax.rem(enc, NX), slot - enc * CAP],
                io_sem.at[3],
            ).start()

    empty = stage.at[pl.ds(0, CAP * owners - images)]
    pltpu.make_async_copy(empty, empty, io_sem.at[2]).wait()
    pltpu.make_async_copy(stage, stage, io_sem.at[3]).wait()
    copies[2].wait()
    copies[3].wait()


def attention(image_counts, gate_logit, token_image, kv, queries, cotangent):
    tokens, hw = queries.shape
    images = 2 * image_counts.shape[0]
    pairs = images // CHUNK + tokens // BLOCK
    vmem = pl.BlockSpec(memory_space=pltpu.VMEM)
    smem = pl.BlockSpec(memory_space=pltpu.SMEM)
    hbm = pl.BlockSpec(memory_space=pltpu.HBM)
    return pl.pallas_call(
        attention_kernel,
        name="attention",
        out_shape=(
            jax.ShapeDtypeStruct((tokens, hw), bf16),
            jax.ShapeDtypeStruct((tokens, hw), bf16),
            jax.ShapeDtypeStruct((2, NZ, NX, CAP, 16, 2 * hw), bf16),
        ),
        in_specs=[smem, smem, vmem, hbm, hbm, hbm],
        out_specs=(hbm, hbm, hbm),
        scratch_shapes=[
            pltpu.VMEM((images, 2, 2, 16, 2 * hw), bf16),
            pltpu.VMEM((images, 2, 2, 16, 2 * hw), bf16),
            pltpu.VMEM((2, 2, 16, 2 * hw), bf16),
            pltpu.VMEM((tokens, hw), bf16),
            pltpu.VMEM((tokens, hw), bf16),
            pltpu.VMEM((tokens, hw), bf16),
            pltpu.VMEM((tokens, hw), bf16),
            pltpu.VMEM((images * 64, 2 * hw), f32),
            pltpu.SMEM((images,), jnp.int32),
            pltpu.SMEM((images + 1,), jnp.int32),
            pltpu.SMEM((pairs,), jnp.int32),
            pltpu.SMEM((pairs,), jnp.int32),
            pltpu.SMEM((pairs,), jnp.int32),
            pltpu.SemaphoreType.DMA((1,)),
            pltpu.SemaphoreType.DMA((6,)),
        ],
        compiler_params=pltpu.CompilerParams(vmem_limit_bytes=62 << 20),
    )(image_counts, gate_logit, token_image.reshape(8, tokens // 8), kv, queries, cotangent)


SCATTER_SEMS = 128


def scatter_kernel(
    gkv_ref, kw_hbm, vw_hbm, theirs_hbm, out_ref,
    weights, mine, theirs, px, py, pz, rx1, rx2, ry1, ry2, zx, zx4, zy, zy4, rz, rz4, tz, lz,
    total, col, col_out, col_in, col_y, out_y, in_y, send_sem, recv_sem, local_sem,
):
    x, y, z, c = place()
    links = Links(send_sem, recv_sem)
    right, left = device(turn(x, 1, NX), y, z, c), device(turn(x, -1, NX), y, z, c)
    north, south = device(x, turn(y, 1, NY), z, c), device(x, turn(y, -1, NY), z, c)
    along = {d: device(x, y, turn(z, d, NZ), c) for d in (-1, 1)}
    other = device(x, y, z, 1 - c)
    hw = kw_hbm.shape[1]
    width = kw_hbm.shape[0]
    nt = (((1,), (1,)), ((), ()))
    greet(x, y, z, c)
    loads = [pltpu.make_async_copy(gkv_ref.at[c], mine, local_sem.at[0])]
    for i, ref in enumerate((kw_hbm, vw_hbm, theirs_hbm.at[0], theirs_hbm.at[1])):
        loads.append(pltpu.make_async_copy(ref, weights.at[i], local_sem.at[1 + i]))
    for copy in loads:
        copy.start()
    meet()
    order = (4, 3, -3, 2, -2, 1, -1, 0)
    at = {k: turn(z, k, NZ) for k in order}
    pieces = {k: links.send(gkv_ref.at[1 - c, at[k]], theirs.at[at[k]], other) for k in order}
    for copy in loads:
        copy.wait()

    def arrive(*copies):
        for copy in copies:
            copy.wait_recv()

    def plus(ref, *arrived):
        value = ref[...].astype(f32)
        for item in arrived:
            value = value + item.astype(f32)
        ref[...] = value.astype(bf16)

    x1, x3, x2 = turn(x, 1, NX), turn(x, -1, NX), turn(x, 2, NX)
    y1, y3, y2 = turn(y, 1, NY), turn(y, -1, NY), turn(y, 2, NY)
    few, many = pl.ds(0, 1), pl.ds(1, 2)
    front, back = pl.ds(0, 2), pl.ds(2, 2)
    n = NX * CAP * 16

    def project(*ks):
        arrive(*[pieces[k] for k in ks])
        data = [ref[at[k]].reshape(n, 2 * hw) for ref in (mine, theirs) for k in ks]
        if len(ks) > 1:
            data = [jnp.concatenate(data[:2], axis=0), jnp.concatenate(data[2:], axis=0)]
        r = None
        for i in range(4):
            a = data[i // 2][:, (i % 2) * hw : (i % 2 + 1) * hw]
            t = lax.dot_general(a, weights[i], nt, preferred_element_type=f32)
            r = t if r is None else r + t
        r = r.astype(bf16)
        for i, k in enumerate(ks):
            part = r[i * n : (i + 1) * n]
            px[at[k]] = part[:, :XCUT].reshape(NX, CAP, 16, XCUT)
            pz[at[k]] = part[:, YCUT:].reshape(NX, CAP, 16, width - YCUT)
            for j in range(NY):
                py[at[k], j] = part[:, XCUT + j * QUARTER : XCUT + (j + 1) * QUARTER].reshape(
                    NX, CAP, 16, QUARTER
                )

    class First:
        def __init__(self, axis, k):
            self.axis, self.k, self.i = axis, k, order.index(k)
            zz = at[k]
            if axis == 0:
                self.cuts = (few, many) if k % 2 else (many, few)
                self.part, self.near, self.far = px.at[zz], (x1, x3), x2
                self.r1, self.r2, self.own = rx1, rx2, x
                self.devs = (right, left)
            else:
                self.cuts = (front, back)
                self.part, self.near, self.far = py.at[zz], (y1, y3), y2
                self.r1, self.r2, self.own = ry1, ry2, y
                self.devs = (north, south)
            self.go = [
                links.send(
                    self.part.at[self.far, self.cuts[s]],
                    self.r1.at[self.i, s, pl.ds(0, self.cuts[s].size)],
                    self.devs[s],
                )
                for s in (0, 1)
            ]

        def forward(self):
            go = []
            for s in (0, 1):
                arrive(self.go[s])
                plus(
                    self.part.at[self.near[s], self.cuts[s]],
                    self.r1[self.i, s, pl.ds(0, self.cuts[s].size)],
                )
                go.append(
                    links.send(self.part.at[self.near[s]], self.r2.at[self.i, s], self.devs[s])
                )
            self.go = go

        def end(self):
            arrive(*self.go)
            plus(self.part.at[self.own], self.r2[self.i, 0], self.r2[self.i, 1])

    def block(axis, k, cut=None):
        ref = (px.at[at[k], x], py.at[at[k], y], pz.at[at[k]])[axis]
        return ref if cut is None else ref.at[cut]

    def zcuts(axis):
        return ((few, many), (pl.ds(0, 3), pl.ds(3, 1)), (front, back))[axis]

    def z_send(axis, k, go):
        land, land4 = ((zx, zx4), (zy, zy4), (rz, rz4))[axis]
        out = []
        for s, d in ((0, 1), (1, -1)):
            cut = zcuts(axis)[s]
            if k == 4:
                out.append(links.send(block(axis, 4, cut), land4.at[s, pl.ds(0, cut.size)], along[d]))
                continue
            arrive(go[s])
            if k == 3:
                plus(block(axis, 3 * d, cut), land4[s, pl.ds(0, cut.size)])
            else:
                plus(block(axis, k * d), land[2 - k, s])
            out.append(links.send(block(axis, k * d), land.at[3 - k, s], along[d]))
        return out

    def z_sum(axis, go):
        land = (zx, zy, rz)[axis]
        arrive(*go)
        value = block(axis, 0)[...].astype(f32)
        for s in (0, 1):
            value = value + land[2, s].astype(f32)
        return value

    def over_x(value, mine_ref, land):
        mine_ref[...] = value.astype(bf16)
        go = []
        for i, d in enumerate((1, 3, 2)):
            xx = turn(x, d, NX)
            go.append(links.send(mine_ref.at[xx], land.at[i], device(xx, y, z, c)))
        return go

    first = {}

    def begin(*ks):
        for k in ks:
            for axis in (1, 0):
                first[axis, k] = First(axis, k)

    def forward(*ks):
        for k in ks:
            for axis in (1, 0):
                first[axis, k].forward()

    def end(*ks):
        for axis in (1, 0):
            for k in ks:
                first[axis, k].end()

    project(4)
    begin(4)
    go_z = z_send(2, 4, None)
    project(3, -3)
    begin(3, -3)
    forward(4)
    go_z = z_send(2, 3, go_z)
    project(2, -2)
    begin(2, -2)
    forward(3, -3)
    end(4)
    go_y, go_x = z_send(1, 4, None), z_send(0, 4, None)
    go_z = z_send(2, 2, go_z)
    project(1, -1)
    begin(1, -1)
    end(3, -3)
    go_y, go_x = z_send(1, 3, go_y), z_send(0, 3, go_x)
    go_z = z_send(2, 1, go_z)
    forward(2, -2)
    project(0)
    begin(0)
    end(2, -2)
    go_y, go_x = z_send(1, 2, go_y), z_send(0, 2, go_x)
    end_z = over_x(z_sum(2, go_z), lz, tz)
    forward(1, -1)
    forward(0)
    end(1, -1)
    go_y, go_x = z_send(1, 1, go_y), z_send(0, 1, go_x)
    end(0)
    value = z_sum(1, go_y)
    for i in range(NX):
        for j in range(NY):
            for p in range(CAP):
                col_y[i, j, 4 * p : 4 * p + 4, :] = value[i, p, 4 * j : 4 * j + 4, :]
            col_y[i, j, 12:16, :] = jnp.zeros((4, QUARTER), f32)
            out_y[i, j] = col_y[i, j].astype(bf16)
    end_y = []
    for i, (dx, dy) in enumerate(STEPS):
        xx, yy = turn(x, dx, NX), turn(y, dy, NY)
        end_y.append(links.send(out_y.at[xx, yy], in_y.at[i], device(xx, yy, z, c)))

    total[:, :, :XCUT] = z_sum(0, go_x)
    arrive(*end_z)
    value = lz[x].astype(f32)
    for i in range(3):
        value = value + tz[i].astype(f32)
    total[:, :, XCUT:] = value
    for j in range(NY):
        for p in range(CAP):
            col[j, 4 * p : 4 * p + 4, :] = total[p, 4 * j : 4 * j + 4, :]
        col[j, 12:16, :] = jnp.zeros((4, total.shape[-1]), f32)
        col_out[j] = col[j].astype(bf16)
    ends = []
    for i, d in enumerate((1, 3, 2)):
        yy = turn(y, d, NY)
        ends.append(links.send(col_out.at[yy], col_in.at[i], device(x, yy, z, c)))
    arrive(*end_y)
    for d in range(NY):
        cols = pl.ds(pl.multiple_of(XCUT + turn(y, -d, NY) * QUARTER, 128), QUARTER)
        terms = [in_y[i].astype(f32) for i, (dx, dy) in enumerate(STEPS) if dy == d]
        if d == 0:
            terms.append(col_y[x, y])
        value = sum(terms[1:], terms[0])
        for p in range(CAP):
            out_ref[p, :, cols] = value[4 * p : 4 * p + 4]
    arrive(*ends)
    result = col[y]
    for i in range(3):
        result = result + col_in[i].astype(f32)
    for p in range(CAP):
        out_ref[p, :, :XCUT] = result[4 * p : 4 * p + 4, :XCUT]
        out_ref[p, :, YCUT:] = result[4 * p : 4 * p + 4, XCUT:]
    links.finish()


def scatter_latents(gkv, kw, vw, theirs):
    width, hw = kw.shape
    rest = width - YCUT
    last = XCUT + rest
    hbm = pl.BlockSpec(memory_space=pltpu.HBM)

    def buffer(*shape):
        return pltpu.VMEM(shape, bf16)

    return pl.pallas_call(
        scatter_kernel,
        name="scatter_latents",
        out_shape=jax.ShapeDtypeStruct((CAP, 4, width), f32),
        in_specs=[hbm, hbm, hbm, hbm],
        out_specs=pl.BlockSpec(memory_space=pltpu.VMEM),
        scratch_shapes=[
            buffer(4, width, hw),
            buffer(NZ, NX, CAP, 16, 2 * hw),
            buffer(NZ, NX, CAP, 16, 2 * hw),
            buffer(NZ, NX, CAP, 16, XCUT),
            buffer(NZ, NY, NX, CAP, 16, QUARTER),
            buffer(NZ, NX, CAP, 16, rest),
            buffer(NZ, 2, 2, 16, XCUT),
            buffer(NZ, 2, CAP, 16, XCUT),
            buffer(NZ, 2, 2, CAP, 16, QUARTER),
            buffer(NZ, 2, NX, CAP, 16, QUARTER),
            buffer(3, 2, CAP, 16, XCUT),
            buffer(2, 2, 16, XCUT),
            buffer(3, 2, NX, CAP, 16, QUARTER),
            buffer(2, 3, CAP, 16, QUARTER),
            buffer(3, 2, NX, CAP, 16, rest),
            buffer(2, 2, CAP, 16, rest),
            buffer(3, CAP, 16, rest),
            buffer(NX, CAP, 16, rest),
            pltpu.VMEM((CAP, 16, last), f32),
            pltpu.VMEM((NY, 16, last), f32),
            buffer(NY, 16, last),
            buffer(3, 16, last),
            pltpu.VMEM((NX, NY, 16, QUARTER), f32),
            buffer(NX, NY, 16, QUARTER),
            buffer(len(STEPS), 16, QUARTER),
            pltpu.SemaphoreType.DMA((SCATTER_SEMS,)),
            pltpu.SemaphoreType.DMA((SCATTER_SEMS,)),
            pltpu.SemaphoreType.DMA((5,)),
        ],
        compiler_params=pltpu.CompilerParams(
            collective_id=1, has_side_effects=True, vmem_limit_bytes=52 << 20
        ),
    )(gkv, kw, vw, theirs)


def on_device(
    latents, key_weight, value_weight, gate_logit, queries, cotangent, image_counts, token_image
):
    kw, vw = key_weight[0], value_weight[0]
    kv, theirs = gather_latents(latents, kw, vw)
    attended, grad_queries, gkv = attention(
        image_counts, gate_logit, token_image, kv, queries[0], cotangent[0]
    )
    grad_latents = scatter_latents(gkv, kw, vw, theirs)
    return attended[None], grad_queries[None], grad_latents


def solution(mesh):
    shards = P("section", None, "enc")
    return jax.shard_map(
        on_device,
        mesh=mesh,
        in_specs=(
            P("enc", "section", None), shards, shards, P("section"), shards, shards, P(), P(),
        ),
        out_specs=(shards, shards, P("enc", "section", None)),
        check_vma=False,
    )
```

```python
import math

import jax
import jax.numpy as jnp
from jax import lax
from jax.experimental import pallas as pl
from jax.experimental.pallas import tpu as pltpu
from jax.sharding import PartitionSpec as P

HD = 128
CAP = 3
NX, NY, NZ = 4, 4, 8
MESH = pl.DeviceIdType.MESH
f32 = jnp.float32
bf16 = jnp.bfloat16


def place():
    section = lax.axis_index("section")
    enc = lax.axis_index("enc")
    x = lax.rem(enc, NX)
    y = lax.rem(section // 2, NY)
    z = (enc // NX) * 2 + section // (2 * NY)
    return x, y, z, lax.rem(section, 2)


def device(x, y, z, c):
    return (lax.rem(z, 2) * (2 * NY) + y * 2 + c, (z // 2) * NX + x)


def turn(a, d, n):
    return lax.rem(a + d + n, n)


class Links:
    def __init__(self, send_sem, recv_sem):
        self.send_sem, self.recv_sem = send_sem, recv_sem
        self.used = 0
        self.sent = []

    def send(self, src, dst, dev):
        i = self.used
        self.used += 1
        copy = pltpu.make_async_remote_copy(
            src_ref=src,
            dst_ref=dst,
            send_sem=self.send_sem.at[i],
            recv_sem=self.recv_sem.at[i],
            device_id=dev,
            device_id_type=MESH,
        )
        copy.start()
        self.sent.append(copy)
        return copy

    def finish(self):
        for copy in self.sent:
            copy.wait_send()


STEPS = [(dx, dy) for dx in range(NX) for dy in range(NY) if dx or dy]


def greet(x, y, z, c):
    peers = [device(turn(x, dx, NX), turn(y, dy, NY), z, c) for dx, dy in STEPS]
    peers += [device(x, y, turn(z, d, NZ), c) for d in (1, -1)]
    peers += [device(x, y, z, 1 - c)]
    barrier = pltpu.get_barrier_semaphore()
    for peer in peers:
        pl.semaphore_signal(barrier, inc=1, device_id=peer, device_id_type=MESH)


def meet():
    pl.semaphore_wait(pltpu.get_barrier_semaphore(), len(STEPS) + 3)


GATHER_SEMS = 160
XCUT, YCUT, QUARTER = 640, 1152, 128


def gather_kernel(
    own_hbm, kw_ref, vw_ref, kv_ref, theirs_ref,
    hx, hy, hz, own, mine, column, rows, out_yz, in_yz, rows_yz, weights, kv, kv_out, send_sem, recv_sem, local_sem,
):
    x, y, z, c = place()
    links = Links(send_sem, recv_sem)
    right, left = device(turn(x, 1, NX), y, z, c), device(turn(x, -1, NX), y, z, c)
    north, south = device(x, turn(y, 1, NY), z, c), device(x, turn(y, -1, NY), z, c)
    along = {d: device(x, y, turn(z, d, NZ), c) for d in (-1, 1)}
    other = device(x, y, z, 1 - c)
    width = own_hbm.shape[-1]
    hw = kw_ref.shape[-1]
    greet(x, y, z, c)
    first = pltpu.make_async_copy(own_hbm, own, local_sem.at[2])
    first.start()
    loads = [
        pltpu.make_async_copy(kw_ref, weights.at[0], local_sem.at[0]),
        pltpu.make_async_copy(vw_ref, weights.at[1], local_sem.at[1]),
    ]
    for copy in loads:
        copy.start()
    first.wait()
    for p in range(CAP):
        mine[4 * p : 4 * p + 4, :] = own[p].astype(f32)
    mine[12:16, :] = jnp.zeros((4, width), f32)
    column[y] = mine[:, :XCUT].astype(bf16)
    for j in range(NY):
        out_yz[j, 0] = mine[:, XCUT + j * QUARTER : XCUT + (j + 1) * QUARTER].astype(bf16)
        out_yz[j, 1] = mine[:, YCUT:].astype(bf16)
    meet()

    firsts = []
    for d in (1, 3, 2):
        firsts.append(links.send(column.at[y], column.at[y], device(x, turn(y, d, NY), z, c)))
    seconds = []
    for dx, dy in STEPS:
        xx, yy = turn(x, dx, NX), turn(y, dy, NY)
        seconds.append(links.send(out_yz.at[yy], in_yz.at[x, y], device(xx, yy, z, c)))
    in_yz[x, y] = out_yz[y]
    for copy in firsts:
        copy.wait_recv()
    for j in range(NY):
        piece = column[j].astype(f32)
        for p in range(CAP):
            rows[p, 4 * j : 4 * j + 4, :] = piece[4 * p : 4 * p + 4, :]
    hx[z, x] = rows[...].astype(bf16)

    def send(ref, dev):
        return links.send(ref, ref, dev)

    def arrive(*copies):
        for copy in copies:
            copy.wait_recv()

    stores = []
    swaps = []

    def store(zz):
        j = 3 + len(stores)
        copy = pltpu.make_async_copy(kv.at[zz], kv_ref.at[c, zz], local_sem.at[j])
        copy.start()
        stores.append(copy)

    def project(zz):
        n = NX * CAP * 16
        data = [hx[zz].reshape(n, XCUT)]
        data += [hy[zz, j].reshape(n, QUARTER) for j in range(NY)]
        data += [hz[zz].reshape(n, width - YCUT)]
        data = jnp.concatenate(data, axis=1)
        for i in (2, 3, 0, 1):
            r = jnp.dot(data, weights[i], preferred_element_type=f32).astype(bf16)
            r = r.reshape(NX, CAP, 16, hw)
            cols = slice((i % 2) * hw, (i % 2 + 1) * hw)
            if i < 2:
                kv[zz, :, :, :, cols] = r
            else:
                kv_out[zz, :, :, :, cols] = r
            if i == 3:
                swaps.append(links.send(kv_out.at[zz], kv_ref.at[c, zz], other))
        store(zz)

    x1, x3 = turn(x, 1, NX), turn(x, -1, NX)
    y1, y3 = turn(y, 1, NY), turn(y, -1, NY)
    few, many = pl.ds(0, 1), pl.ds(1, 2)
    front, back = pl.ds(0, 2), pl.ds(2, 2)

    class Last:
        def __init__(self, axis, k):
            self.axis, self.k, self.zz = axis, k, turn(z, k, NZ)
            if axis == 0:
                self.go = [send(hx.at[self.zz, x], dev) for dev in (right, left)]
            else:
                self.go = [send(hy.at[self.zz, y], dev) for dev in (north, south)]

        def forward(self):
            a, b = self.go
            if self.axis == 0:
                sa, sb = (few, many) if self.k % 2 else (many, few)
                arrive(a)
                a = send(hx.at[self.zz, x3, sa], right)
                arrive(b)
                b = send(hx.at[self.zz, x1, sb], left)
            else:
                arrive(a)
                a = send(hy.at[self.zz, y3, front], north)
                arrive(b)
                b = send(hy.at[self.zz, y1, back], south)
            self.go = [a, b]

        def end(self):
            arrive(*self.go)

    def block(axis, k, cut=None):
        zz = turn(z, k, NZ)
        ref = (hx.at[zz, x], hy.at[zz, y], hz.at[zz])[axis]
        return ref if cut is None else ref.at[cut]

    def over_z(axis):
        return [send(block(axis, 0), along[1]), send(block(axis, 0), along[-1])]

    def pass_on(axis, s, go):
        cuts = ((few, many), (pl.ds(0, 3), pl.ds(3, 1)), (front, back))[axis]
        out = []
        for i, d in ((0, -s), (1, s)):
            arrive(go[i])
            if s < 4:
                out.append(send(block(axis, d, cuts[i] if s == 3 else None), along[1 - 2 * i]))
        if axis < 2:
            for d in (-s, s) if s < 4 else (4,):
                last[axis, d] = Last(axis, d)
        return out

    for copy in loads:
        copy.wait()
    go_x = over_z(0)
    swap_w = [links.send(weights.at[i], weights.at[2 + i], other) for i in (0, 1)]
    last = {(0, 0): Last(0, 0)}
    arrive(*seconds)
    for i in range(NX):
        for j in range(NY):
            piece = in_yz[i, j].astype(f32)
            for p in range(CAP):
                for s in range(2):
                    rows_yz[s, p, 4 * j : 4 * j + 4, :] = piece[s, 4 * p : 4 * p + 4, :]
        hy[z, y, i] = rows_yz[0].astype(bf16)
        hz[z, i] = rows_yz[1].astype(bf16)
    go_y = over_z(1)
    last[1, 0] = Last(1, 0)
    go_z = over_z(2)

    def finish(k):
        project(turn(z, k, NZ))

    arrive(*swap_w)
    theirs = pltpu.make_async_copy(weights.at[pl.ds(2, 2)], theirs_ref, local_sem.at[2])
    theirs.start()

    def forward(*ks):
        for axis in (0, 1):
            for k in ks:
                last[axis, k].forward()

    def end(*ks):
        for axis in (0, 1):
            for k in ks:
                last[axis, k].end()

    go_x = pass_on(0, 1, go_x)
    go_y = pass_on(1, 1, go_y)
    go_z = pass_on(2, 1, go_z)
    forward(0)
    go_x = pass_on(0, 2, go_x)
    go_y = pass_on(1, 2, go_y)
    go_z = pass_on(2, 2, go_z)
    forward(1, -1)
    end(0)
    go_x = pass_on(0, 3, go_x)
    go_y = pass_on(1, 3, go_y)
    go_z = pass_on(2, 3, go_z)
    forward(2, -2)
    finish(0)
    end(1, -1)
    pass_on(0, 4, go_x)
    pass_on(1, 4, go_y)
    pass_on(2, 4, go_z)
    finish(1)
    forward(3, -3)
    finish(-1)
    end(2, -2)
    forward(4)
    finish(2)
    finish(-2)
    end(3, -3)
    finish(3)
    finish(-3)
    end(4)
    finish(4)

    arrive(*swaps)
    theirs.wait()
    for copy in stores:
        copy.wait()
    links.finish()


def gather_latents(latents, key_weight, value_weight):
    width = latents.shape[2]
    hw = key_weight.shape[1]
    hbm = pl.BlockSpec(memory_space=pltpu.HBM)
    return pl.pallas_call(
        gather_kernel,
        name="gather_latents",
        out_shape=(
            jax.ShapeDtypeStruct((2, NZ, NX, CAP, 16, 2 * hw), bf16),
            jax.ShapeDtypeStruct((2,) + key_weight.shape, bf16),
        ),
        in_specs=[hbm, hbm, hbm],
        out_specs=(hbm, hbm),
        scratch_shapes=[
            pltpu.VMEM((NZ, NX, CAP, 16, XCUT), bf16),
            pltpu.VMEM((NZ, NY, NX, CAP, 16, QUARTER), bf16),
            pltpu.VMEM((NZ, NX, CAP, 16, width - YCUT), bf16),
            pltpu.VMEM(latents.shape, bf16),
            pltpu.VMEM((16, width), f32),
            pltpu.VMEM((NY, 16, XCUT), bf16),
            pltpu.VMEM((CAP, 16, XCUT), f32),
            pltpu.VMEM((NY, 2, 16, QUARTER), bf16),
            pltpu.VMEM((NX, NY, 2, 16, QUARTER), bf16),
            pltpu.VMEM((2, CAP, 16, QUARTER), f32),
            pltpu.VMEM((4,) + key_weight.shape, bf16),
            pltpu.VMEM((NZ, NX, CAP, 16, 2 * hw), bf16),
            pltpu.VMEM((NZ, NX, CAP, 16, 2 * hw), bf16),
            pltpu.SemaphoreType.DMA((GATHER_SEMS,)),
            pltpu.SemaphoreType.DMA((GATHER_SEMS,)),
            pltpu.SemaphoreType.DMA((3 + NZ,)),
        ],
        compiler_params=pltpu.CompilerParams(
            collective_id=0, has_side_effects=True, vmem_limit_bytes=62 << 20
        ),
    )(latents, key_weight, value_weight)


BLOCK = 128
CHUNK = 4
SIDE = 5


def attention_kernel(
    counts_ref, gate_ref, token_ref, kv_ref, q_hbm, cot_hbm,
    att_hbm, gq_hbm, gkv_ref,
    kvs, stage, zeros, q_ref, cot_ref, att_ref, gq_ref, gacc,
    slots, starts, chunk_of, block_of, begin_of, sem, io_sem,
):
    owners = counts_ref.shape[0]
    images = 2 * owners
    chunks = images // CHUNK
    heads = q_ref.shape[1] // HD
    hw = heads * HD
    scale = 1.0 / math.sqrt(HD)
    cols = CHUNK * 64
    tokens = q_ref.shape[0]
    pairs = chunk_of.shape[0]
    nt = (((1,), (1,)), ((), ()))

    copies = [
        pltpu.make_async_copy(q_hbm, q_ref, io_sem.at[0]),
        pltpu.make_async_copy(cot_hbm, cot_ref, io_sem.at[1]),
        pltpu.make_async_copy(att_ref, att_hbm, io_sem.at[4]),
        pltpu.make_async_copy(gq_ref, gq_hbm, io_sem.at[5]),
    ]
    zeros[...] = jnp.zeros_like(zeros)
    n = 0
    for e in range(owners):
        count = counts_ref[e]
        x, zs = e % NX, pl.ds(2 * (e // NX), 2)
        for p in range(CAP):

            @pl.when(p < count)
            def _():
                slots[n + p] = e * CAP + p
                pltpu.make_async_copy(kv_ref.at[:, zs, x, p], kvs.at[n + p], sem.at[0]).start()

            @pl.when(p >= count)
            def _():
                pltpu.make_async_copy(zeros, gkv_ref.at[:, zs, x, p], io_sem.at[2]).start()

        n = n + count
        if e == 1:
            copies[0].start()
            copies[1].start()
    token_image = token_ref[...]
    for i in range(images + 1):
        starts[i] = jnp.sum((token_image < i).astype(jnp.int32))
    factor = jnp.tanh(jnp.full((1, HD), gate_ref[0], f32))
    for i in range(pairs):
        chunk_of[i] = 0
        block_of[i] = 0
        begin_of[i] = tokens
    n = 0
    for q in range(chunks):
        b0 = starts[q * CHUNK] // BLOCK
        b1 = (starts[(q + 1) * CHUNK] + BLOCK - 1) // BLOCK

        @pl.loop(b0, b1)
        def _(b):
            i = n + b - b0
            chunk_of[i] = q
            block_of[i] = b
            begin_of[i] = b * BLOCK

        n = n + b1 - b0
    gacc[...] = jnp.zeros_like(gacc)
    copies[0].wait()
    copies[1].wait()
    pltpu.make_async_copy(kvs, kvs, sem.at[0]).wait()

    @pl.loop(0, (n + SIDE - 1) // SIDE)
    def _(step):
        work = []
        for u in range(SIDE):
            i = step * SIDE + u
            q, b, begin = chunk_of[i], block_of[i], begin_of[i]
            four = pl.ds(q * CHUNK, CHUNK)
            trows = pl.ds(pl.multiple_of(b * BLOCK, BLOCK), BLOCK)
            krows = pl.ds(pl.multiple_of(q * cols, cols), cols)
            edges = [starts[q * CHUNK + j] for j in range(CHUNK + 1)]
            which = lax.broadcasted_iota(jnp.int32, (1, cols), 1) // 64
            first = jnp.full((1, cols), edges[0], jnp.int32)
            last = jnp.full((1, cols), edges[1], jnp.int32)
            for j in range(1, CHUNK):
                first = jnp.where(which == j, edges[j], first)
                last = jnp.where(which == j, edges[j + 1], last)
            token = lax.broadcasted_iota(jnp.int32, (BLOCK, 1), 0) + begin
            here = jnp.logical_and(token >= edges[0], token < edges[CHUNK])
            wide = jnp.logical_and(token >= first, token < last).astype(f32).astype(bf16)
            lane = lax.broadcasted_iota(jnp.int32, (1, BLOCK), 1) + begin
            tall = [
                jnp.logical_and(lane >= edges[j], lane < edges[j + 1]) for j in range(CHUNK)
            ]
            ones = [t.astype(f32).astype(bf16) for t in tall]
            for h in range(heads):
                hc = slice(h * HD, (h + 1) * HD)
                vc = slice(hw + h * HD, hw + (h + 1) * HD)
                qb = q_ref[trows, hc]
                k = kvs[four, :, :, :, hc].reshape(cols, HD)
                v = kvs[four, :, :, :, vc].reshape(cols, HD)
                gm = (factor * cot_ref[trows, hc].astype(f32)).astype(bf16)
                s = lax.dot_general(k, qb, nt, preferred_element_type=f32)
                gp = lax.dot_general(v, gm, nt, preferred_element_type=f32)
                work.append((hc, vc, trows, krows, here, wide, tall, ones, qb, k, v, gm, s, gp))

        def pick(full, tall):
            out = full[(CHUNK - 1) * 64 :]
            for j in range(CHUNK - 1):
                out = jnp.where(tall[j], full[j * 64 : (j + 1) * 64], out)
            return out

        def spread(small, ones, wide):
            rows = small.astype(bf16)
            down = jnp.concatenate([rows * ones[j] for j in range(CHUNK)], axis=0)
            twice = jnp.concatenate([small, small], axis=0).T.astype(bf16)
            return down, jnp.concatenate([twice] * (CHUNK // 2), axis=1) * wide

        done = []
        for hc, vc, trows, krows, here, wide, tall, ones, qb, k, v, gm, s, gp in work:
            s = pick(s, tall)
            gp = pick(gp, tall)
            e = jnp.exp((s - jnp.max(s, axis=0, keepdims=True)) * scale)
            p = e * (1.0 / jnp.sum(e, axis=0, keepdims=True))
            w = jnp.sum(p * gp, axis=0, keepdims=True)
            gs = p * (gp - w) * scale
            p_down, p_wide = spread(p, ones, wide)
            gs_down, gs_wide = spread(gs, ones, wide)
            done.append((
                jnp.dot(p_wide, v, preferred_element_type=f32),
                jnp.dot(gs_wide, k, preferred_element_type=f32),
                jnp.dot(gs_down, qb, preferred_element_type=f32),
                jnp.dot(p_down, gm, preferred_element_type=f32),
            ))
        for item, (mix, gq, gk, gv) in zip(work, done):
            hc, vc, trows, krows, here = item[:5]
            att_ref[trows, hc] = jnp.where(here, (factor * mix).astype(bf16), att_ref[trows, hc])
            gq_ref[trows, hc] = jnp.where(here, gq.astype(bf16), gq_ref[trows, hc])
            gacc[krows, hc] += gk
            gacc[krows, vc] += gv

    copies[2].start()
    copies[3].start()

    @pl.loop(0, chunks)
    def _(q):
        krows = pl.ds(pl.multiple_of(q * cols, cols), cols)
        stage[pl.ds(q * CHUNK, CHUNK)] = (
            gacc[krows, :].astype(bf16).reshape(CHUNK, 2, 2, 16, 2 * hw)
        )
        for j in range(CHUNK):
            i = q * CHUNK + j
            slot = slots[i]
            enc = slot // CAP
            pltpu.make_async_copy(
                stage.at[i],
                gkv_ref.at[:, pl.ds(2 * (enc // NX), 2), lax.rem(enc, NX), slot - enc * CAP],
                io_sem.at[3],
            ).start()

    empty = stage.at[pl.ds(0, CAP * owners - images)]
    pltpu.make_async_copy(empty, empty, io_sem.at[2]).wait()
    pltpu.make_async_copy(stage, stage, io_sem.at[3]).wait()
    copies[2].wait()
    copies[3].wait()


def attention(image_counts, gate_logit, token_image, kv, queries, cotangent):
    tokens, hw = queries.shape
    images = 2 * image_counts.shape[0]
    pairs = images // CHUNK + tokens // BLOCK
    vmem = pl.BlockSpec(memory_space=pltpu.VMEM)
    smem = pl.BlockSpec(memory_space=pltpu.SMEM)
    hbm = pl.BlockSpec(memory_space=pltpu.HBM)
    return pl.pallas_call(
        attention_kernel,
        name="attention",
        out_shape=(
            jax.ShapeDtypeStruct((tokens, hw), bf16),
            jax.ShapeDtypeStruct((tokens, hw), bf16),
            jax.ShapeDtypeStruct((2, NZ, NX, CAP, 16, 2 * hw), bf16),
        ),
        in_specs=[smem, smem, vmem, hbm, hbm, hbm],
        out_specs=(hbm, hbm, hbm),
        scratch_shapes=[
            pltpu.VMEM((images, 2, 2, 16, 2 * hw), bf16),
            pltpu.VMEM((images, 2, 2, 16, 2 * hw), bf16),
            pltpu.VMEM((2, 2, 16, 2 * hw), bf16),
            pltpu.VMEM((tokens, hw), bf16),
            pltpu.VMEM((tokens, hw), bf16),
            pltpu.VMEM((tokens, hw), bf16),
            pltpu.VMEM((tokens, hw), bf16),
            pltpu.VMEM((images * 64, 2 * hw), f32),
            pltpu.SMEM((images,), jnp.int32),
            pltpu.SMEM((images + 1,), jnp.int32),
            pltpu.SMEM((pairs,), jnp.int32),
            pltpu.SMEM((pairs,), jnp.int32),
            pltpu.SMEM((pairs,), jnp.int32),
            pltpu.SemaphoreType.DMA((1,)),
            pltpu.SemaphoreType.DMA((6,)),
        ],
        compiler_params=pltpu.CompilerParams(vmem_limit_bytes=62 << 20),
    )(image_counts, gate_logit, token_image.reshape(8, tokens // 8), kv, queries, cotangent)


SCATTER_SEMS = 128


def scatter_kernel(
    gkv_ref, kw_hbm, vw_hbm, theirs_hbm, out_ref,
    weights, mine, theirs, px, py, pz, rx1, rx2, ry1, ry2, zx, zx4, zy, zy4, rz, rz4, tz, lz,
    total, col, col_out, col_in, col_y, out_y, in_y, send_sem, recv_sem, local_sem,
):
    x, y, z, c = place()
    links = Links(send_sem, recv_sem)
    right, left = device(turn(x, 1, NX), y, z, c), device(turn(x, -1, NX), y, z, c)
    north, south = device(x, turn(y, 1, NY), z, c), device(x, turn(y, -1, NY), z, c)
    along = {d: device(x, y, turn(z, d, NZ), c) for d in (-1, 1)}
    other = device(x, y, z, 1 - c)
    hw = kw_hbm.shape[1]
    width = kw_hbm.shape[0]
    nt = (((1,), (1,)), ((), ()))
    greet(x, y, z, c)
    loads = [pltpu.make_async_copy(gkv_ref.at[c], mine, local_sem.at[0])]
    for i, ref in enumerate((kw_hbm, vw_hbm, theirs_hbm.at[0], theirs_hbm.at[1])):
        loads.append(pltpu.make_async_copy(ref, weights.at[i], local_sem.at[1 + i]))
    for copy in loads:
        copy.start()
    meet()
    order = (4, 3, -3, 2, -2, 1, -1, 0)
    at = {k: turn(z, k, NZ) for k in order}
    pieces = {k: links.send(gkv_ref.at[1 - c, at[k]], theirs.at[at[k]], other) for k in order}
    for copy in loads:
        copy.wait()

    def arrive(*copies):
        for copy in copies:
            copy.wait_recv()

    def plus(ref, *arrived):
        value = ref[...].astype(f32)
        for item in arrived:
            value = value + item.astype(f32)
        ref[...] = value.astype(bf16)

    x1, x3, x2 = turn(x, 1, NX), turn(x, -1, NX), turn(x, 2, NX)
    y1, y3, y2 = turn(y, 1, NY), turn(y, -1, NY), turn(y, 2, NY)
    few, many = pl.ds(0, 1), pl.ds(1, 2)
    front, back = pl.ds(0, 2), pl.ds(2, 2)
    n = NX * CAP * 16

    def project(*ks):
        arrive(*[pieces[k] for k in ks])
        data = [ref[at[k]].reshape(n, 2 * hw) for ref in (mine, theirs) for k in ks]
        if len(ks) > 1:
            data = [jnp.concatenate(data[:2], axis=0), jnp.concatenate(data[2:], axis=0)]
        r = None
        for i in range(4):
            a = data[i // 2][:, (i % 2) * hw : (i % 2 + 1) * hw]
            t = lax.dot_general(a, weights[i], nt, preferred_element_type=f32)
            r = t if r is None else r + t
        r = r.astype(bf16)
        for i, k in enumerate(ks):
            part = r[i * n : (i + 1) * n]
            px[at[k]] = part[:, :XCUT].reshape(NX, CAP, 16, XCUT)
            pz[at[k]] = part[:, YCUT:].reshape(NX, CAP, 16, width - YCUT)
            for j in range(NY):
                py[at[k], j] = part[:, XCUT + j * QUARTER : XCUT + (j + 1) * QUARTER].reshape(
                    NX, CAP, 16, QUARTER
                )

    class First:
        def __init__(self, axis, k):
            self.axis, self.k, self.i = axis, k, order.index(k)
            zz = at[k]
            if axis == 0:
                self.cuts = (few, many) if k % 2 else (many, few)
                self.part, self.near, self.far = px.at[zz], (x1, x3), x2
                self.r1, self.r2, self.own = rx1, rx2, x
                self.devs = (right, left)
            else:
                self.cuts = (front, back)
                self.part, self.near, self.far = py.at[zz], (y1, y3), y2
                self.r1, self.r2, self.own = ry1, ry2, y
                self.devs = (north, south)
            self.go = [
                links.send(
                    self.part.at[self.far, self.cuts[s]],
                    self.r1.at[self.i, s, pl.ds(0, self.cuts[s].size)],
                    self.devs[s],
                )
                for s in (0, 1)
            ]

        def forward(self):
            go = []
            for s in (0, 1):
                arrive(self.go[s])
                plus(
                    self.part.at[self.near[s], self.cuts[s]],
                    self.r1[self.i, s, pl.ds(0, self.cuts[s].size)],
                )
                go.append(
                    links.send(self.part.at[self.near[s]], self.r2.at[self.i, s], self.devs[s])
                )
            self.go = go

        def end(self):
            arrive(*self.go)
            plus(self.part.at[self.own], self.r2[self.i, 0], self.r2[self.i, 1])

    def block(axis, k, cut=None):
        ref = (px.at[at[k], x], py.at[at[k], y], pz.at[at[k]])[axis]
        return ref if cut is None else ref.at[cut]

    def zcuts(axis):
        return ((few, many), (pl.ds(0, 3), pl.ds(3, 1)), (front, back))[axis]

    def z_send(axis, k, go):
        land, land4 = ((zx, zx4), (zy, zy4), (rz, rz4))[axis]
        out = []
        for s, d in ((0, 1), (1, -1)):
            cut = zcuts(axis)[s]
            if k == 4:
                out.append(links.send(block(axis, 4, cut), land4.at[s, pl.ds(0, cut.size)], along[d]))
                continue
            arrive(go[s])
            if k == 3:
                plus(block(axis, 3 * d, cut), land4[s, pl.ds(0, cut.size)])
            else:
                plus(block(axis, k * d), land[2 - k, s])
            out.append(links.send(block(axis, k * d), land.at[3 - k, s], along[d]))
        return out

    def z_sum(axis, go):
        land = (zx, zy, rz)[axis]
        arrive(*go)
        value = block(axis, 0)[...].astype(f32)
        for s in (0, 1):
            value = value + land[2, s].astype(f32)
        return value

    def over_x(value, mine_ref, land):
        mine_ref[...] = value.astype(bf16)
        go = []
        for i, d in enumerate((1, 3, 2)):
            xx = turn(x, d, NX)
            go.append(links.send(mine_ref.at[xx], land.at[i], device(xx, y, z, c)))
        return go

    first = {}

    def begin(*ks):
        for k in ks:
            for axis in (1, 0):
                first[axis, k] = First(axis, k)

    def forward(*ks):
        for k in ks:
            for axis in (1, 0):
                first[axis, k].forward()

    def end(*ks):
        for axis in (1, 0):
            for k in ks:
                first[axis, k].end()

    project(4)
    begin(4)
    go_z = z_send(2, 4, None)
    project(3, -3)
    begin(3, -3)
    forward(4)
    go_z = z_send(2, 3, go_z)
    project(2, -2)
    begin(2, -2)
    forward(3, -3)
    end(4)
    go_y, go_x = z_send(1, 4, None), z_send(0, 4, None)
    go_z = z_send(2, 2, go_z)
    project(1, -1)
    begin(1, -1)
    end(3, -3)
    go_y, go_x = z_send(1, 3, go_y), z_send(0, 3, go_x)
    go_z = z_send(2, 1, go_z)
    forward(2, -2)
    project(0)
    begin(0)
    end(2, -2)
    go_y, go_x = z_send(1, 2, go_y), z_send(0, 2, go_x)
    end_z = over_x(z_sum(2, go_z), lz, tz)
    forward(1, -1)
    forward(0)
    end(1, -1)
    go_y, go_x = z_send(1, 1, go_y), z_send(0, 1, go_x)
    end(0)
    value = z_sum(1, go_y)
    for i in range(NX):
        for j in range(NY):
            for p in range(CAP):
                col_y[i, j, 4 * p : 4 * p + 4, :] = value[i, p, 4 * j : 4 * j + 4, :]
            col_y[i, j, 12:16, :] = jnp.zeros((4, QUARTER), f32)
            out_y[i, j] = col_y[i, j].astype(bf16)
    end_y = []
    for i, (dx, dy) in enumerate(STEPS):
        xx, yy = turn(x, dx, NX), turn(y, dy, NY)
        end_y.append(links.send(out_y.at[xx, yy], in_y.at[i], device(xx, yy, z, c)))

    total[:, :, :XCUT] = z_sum(0, go_x)
    arrive(*end_z)
    value = lz[x].astype(f32)
    for i in range(3):
        value = value + tz[i].astype(f32)
    total[:, :, XCUT:] = value
    for j in range(NY):
        for p in range(CAP):
            col[j, 4 * p : 4 * p + 4, :] = total[p, 4 * j : 4 * j + 4, :]
        col[j, 12:16, :] = jnp.zeros((4, total.shape[-1]), f32)
        col_out[j] = col[j].astype(bf16)
    ends = []
    for i, d in enumerate((1, 3, 2)):
        yy = turn(y, d, NY)
        ends.append(links.send(col_out.at[yy], col_in.at[i], device(x, yy, z, c)))
    arrive(*end_y)
    for d in range(NY):
        cols = pl.ds(pl.multiple_of(XCUT + turn(y, -d, NY) * QUARTER, 128), QUARTER)
        terms = [in_y[i].astype(f32) for i, (dx, dy) in enumerate(STEPS) if dy == d]
        if d == 0:
            terms.append(col_y[x, y])
        value = sum(terms[1:], terms[0])
        for p in range(CAP):
            out_ref[p, :, cols] = value[4 * p : 4 * p + 4]
    arrive(*ends)
    result = col[y]
    for i in range(3):
        result = result + col_in[i].astype(f32)
    for p in range(CAP):
        out_ref[p, :, :XCUT] = result[4 * p : 4 * p + 4, :XCUT]
        out_ref[p, :, YCUT:] = result[4 * p : 4 * p + 4, XCUT:]
    links.finish()


def scatter_latents(gkv, kw, vw, theirs):
    width, hw = kw.shape
    rest = width - YCUT
    last = XCUT + rest
    hbm = pl.BlockSpec(memory_space=pltpu.HBM)

    def buffer(*shape):
        return pltpu.VMEM(shape, bf16)

    return pl.pallas_call(
        scatter_kernel,
        name="scatter_latents",
        out_shape=jax.ShapeDtypeStruct((CAP, 4, width), f32),
        in_specs=[hbm, hbm, hbm, hbm],
        out_specs=pl.BlockSpec(memory_space=pltpu.VMEM),
        scratch_shapes=[
            buffer(4, width, hw),
            buffer(NZ, NX, CAP, 16, 2 * hw),
            buffer(NZ, NX, CAP, 16, 2 * hw),
            buffer(NZ, NX, CAP, 16, XCUT),
            buffer(NZ, NY, NX, CAP, 16, QUARTER),
            buffer(NZ, NX, CAP, 16, rest),
            buffer(NZ, 2, 2, 16, XCUT),
            buffer(NZ, 2, CAP, 16, XCUT),
            buffer(NZ, 2, 2, CAP, 16, QUARTER),
            buffer(NZ, 2, NX, CAP, 16, QUARTER),
            buffer(3, 2, CAP, 16, XCUT),
            buffer(2, 2, 16, XCUT),
            buffer(3, 2, NX, CAP, 16, QUARTER),
            buffer(2, 3, CAP, 16, QUARTER),
            buffer(3, 2, NX, CAP, 16, rest),
            buffer(2, 2, CAP, 16, rest),
            buffer(3, CAP, 16, rest),
            buffer(NX, CAP, 16, rest),
            pltpu.VMEM((CAP, 16, last), f32),
            pltpu.VMEM((NY, 16, last), f32),
            buffer(NY, 16, last),
            buffer(3, 16, last),
            pltpu.VMEM((NX, NY, 16, QUARTER), f32),
            buffer(NX, NY, 16, QUARTER),
            buffer(len(STEPS), 16, QUARTER),
            pltpu.SemaphoreType.DMA((SCATTER_SEMS,)),
            pltpu.SemaphoreType.DMA((SCATTER_SEMS,)),
            pltpu.SemaphoreType.DMA((5,)),
        ],
        compiler_params=pltpu.CompilerParams(
            collective_id=1, has_side_effects=True, vmem_limit_bytes=52 << 20
        ),
    )(gkv, kw, vw, theirs)


def on_device(
    latents, key_weight, value_weight, gate_logit, queries, cotangent, image_counts, token_image
):
    kw, vw = key_weight[0], value_weight[0]
    kv, theirs = gather_latents(latents, kw, vw)
    attended, grad_queries, gkv = attention(
        image_counts, gate_logit, token_image, kv, queries[0], cotangent[0]
    )
    grad_latents = scatter_latents(gkv, kw, vw, theirs)
    return attended[None], grad_queries[None], grad_latents


def solution(mesh):
    shards = P("section", None, "enc")
    return jax.shard_map(
        on_device,
        mesh=mesh,
        in_specs=(
            P("enc", "section", None), shards, shards, P("section"), shards, shards, P(), P(),
        ),
        out_specs=(shards, shards, P("enc", "section", None)),
        check_vma=False,
    )
```
